128 devices in a mesh: row: 4 (over x), col: 8 (over y_lo, z), depth: 4 (over y_hi, core).
Axes of the slice: x: 4, y: 4 (y_hi: 2, y_lo: 2; y = y_hi * 2 + y_lo), z: 4, core: 2. Of those that a mesh axis runs over, the one named last changes fastest.
Arguments:
- inputs: bfloat16 [20480, 1664], P(('row', 'col', 'depth')), may hold values from -6 to 6
- upstream: bfloat16 [20480, 1664], P(('row', 'col', 'depth')), may hold values from -6 to 6
- norm_gain: float32 [1664], replicated, may hold values from 0.5 to 1.5
- norm_shift: float32 [1664], replicated, may hold values from -3 to 3
- expand_weight: bfloat16 [1664, 8192], P(('row', 'depth'), 'col'), may hold values from -0.15625 to 0.15625
- expand_bias: float32 [8192], P('col'), may hold values from -3 to 3
- shrink_weight: bfloat16 [1664, 8192], P(('row', 'depth'), 'col'), may hold values from -0.0625 to 0.0625
Outputs:
- inputs_grad: bfloat16 [20480, 1664], P(('row', 'col', 'depth'))
- gain_grad: float32 [1664], replicated
- shift_grad: float32 [1664], replicated
- expand_grad: float32 [1664, 8192], P(('row', 'depth'), 'col')
- bias_grad: float32 [8192], P('col')
- shrink_grad: float32 [1664, 8192], P(('row', 'depth'), 'col')
The draws below stay inside these ranges and needn't reach their ends.
All inputs are finite; a program needn't handle non-finite values.
Results may differ from the reference program's by a relative error of at most 0.007.
Values may be sent and summed in bfloat16 or wider, within the bound.
No kernel may reach another device: no remote copies, remote signals or barrier semaphores. Data moves between devices by JAX's collectives and lax.ppermute only.
A program may use at most 128 MiB of HBM per device.

```python
import jax
import jax.numpy as jnp
from jax import lax

D = 1664
FF = 8192
TOK_DEV = 1280
TOKENS = 20480
N_ROW = 4
N_DEPTH = 4


def level_of(own_key, dims, pieces, low, largest):
    level = 1.0
    for position, parts in pieces:
        steps = jax.random.uniform(jax.random.fold_in(jax.random.fold_in(own_key, 6), position), (parts,), jnp.float32, low / len(pieces), largest / len(pieces))
        level = level * jnp.repeat(jnp.exp(steps), dims[position] // parts).reshape((-1,) + (1,) * (len(dims) - 1 - position))
    return level


def normal_values(rng, dims, deviation, reach, shards=(), held_as=jnp.bfloat16):
    entries = deviation * jax.random.normal(rng, dims, jnp.float32)
    if shards:
        entries = entries * level_of(rng, dims, shards, -0.22, 0.18)
    return jnp.clip(entries, -reach, reach).astype(held_as)


def setup_inputs(seed: int = 0) -> dict:
    keys = jax.random.split(jax.random.key(seed), 8)
    inputs = normal_values(keys[0], (TOKENS, D), 1.0, 6.0, ((0, 128),))
    upstream = normal_values(keys[1], (TOKENS, D), 1.0, 6.0, ((0, 128),))
    norm_gain = jnp.clip(1.0 + 0.1 * jax.random.normal(keys[2], (D,), jnp.float32), 0.5, 1.5)
    norm_shift = normal_values(keys[3], (D,), 0.5, 3.0, (), jnp.float32)
    expand_weight = normal_values(keys[4], (D, FF), D ** -0.5, 0.15625, ((0, 16), (1, 8)))
    expand_bias = normal_values(keys[5], (FF,), 0.5, 3.0, ((0, 8),), jnp.float32)
    shrink_weight = normal_values(keys[6], (D, FF), FF ** -0.5, 0.0625, ((0, 16), (1, 8)))
    return dict(inputs=inputs, upstream=upstream, norm_gain=norm_gain, norm_shift=norm_shift, expand_weight=expand_weight, expand_bias=expand_bias, shrink_weight=shrink_weight)


epsilon = 1e-06
root_half = 0.7071067811865476
inv_root_two_pi = 0.3989422804014327

def gelu_parts(pre):
    cdf = 0.5 * (1.0 + lax.erf(pre * root_half))
    density = inv_root_two_pi * jnp.exp(-0.5 * pre * pre)
    return (pre * cdf, cdf + pre * density)

def reference(inputs, upstream, norm_gain, norm_shift, expand_weight, expand_bias, shrink_weight):
    blocks = N_ROW * N_DEPTH

    def block_step(carry, index):
        expand_acc, shrink_acc, bias_acc, gain_acc, shift_acc = carry
        start = (index * TOK_DEV).astype(jnp.int32)
        rows_in = lax.dynamic_slice_in_dim(inputs, start, TOK_DEV, 0)
        rows_up = lax.dynamic_slice_in_dim(upstream, start, TOK_DEV, 0)
        features = rows_in.astype(jnp.float32)
        centre = lax.optimization_barrier(jnp.mean(features, axis=1, keepdims=True))
        shifted = features - centre
        scale_inv = lax.rsqrt(lax.optimization_barrier(jnp.mean(shifted * shifted, axis=1, keepdims=True)) + epsilon)
        normed = shifted * scale_inv
        normed_bf = (normed * norm_gain + norm_shift).astype(jnp.bfloat16)
        pre = jnp.dot(normed_bf, expand_weight, preferred_element_type=jnp.float32) + expand_bias
        activated, slope = gelu_parts(pre)
        activated = activated.astype(jnp.bfloat16)
        back_act = jnp.dot(rows_up, shrink_weight, preferred_element_type=jnp.float32)
        back_pre = (back_act * slope).astype(jnp.bfloat16)
        shrink_acc = shrink_acc + jnp.dot(rows_up.T, activated, preferred_element_type=jnp.float32)
        expand_acc = expand_acc + jnp.dot(normed_bf.T, back_pre, preferred_element_type=jnp.float32)
        bias_acc = bias_acc + lax.optimization_barrier(jnp.sum(back_pre.astype(jnp.float32), axis=0))
        grad_normed = jnp.dot(back_pre, expand_weight.T, preferred_element_type=jnp.float32)
        weighted = grad_normed * norm_gain
        mean_one = lax.optimization_barrier(jnp.mean(weighted, axis=1, keepdims=True))
        mean_two = lax.optimization_barrier(jnp.mean(weighted * normed, axis=1, keepdims=True))
        result = scale_inv * (weighted - mean_one - normed * mean_two)
        grad_rows = (rows_up.astype(jnp.float32) + result).astype(jnp.bfloat16)
        gain_acc = gain_acc + lax.optimization_barrier(jnp.sum(grad_normed * normed, axis=0))
        shift_acc = shift_acc + lax.optimization_barrier(jnp.sum(grad_normed, axis=0))
        return ((expand_acc, shrink_acc, bias_acc, gain_acc, shift_acc), grad_rows)
    start_carry = (jnp.zeros((D, FF), jnp.float32), jnp.zeros((D, FF), jnp.float32), jnp.zeros((FF,), jnp.float32), jnp.zeros((D,), jnp.float32), jnp.zeros((D,), jnp.float32))
    final, grad_blocks = lax.scan(block_step, start_carry, jnp.arange(blocks, dtype=jnp.int32))
    expand_grad, shrink_grad, bias_grad, gain_grad, shift_grad = final
    inputs_grad = grad_blocks.reshape(TOKENS, D)
    return (inputs_grad, gain_grad, shift_grad, expand_grad, bias_grad, shrink_grad)
```

```python
import jax
import jax.numpy as jnp
from jax import lax
from jax.sharding import Mesh, PartitionSpec as P

EPSILON = 1e-06
ROOT_HALF = 0.7071067811865476
INV_ROOT_TWO_PI = 0.3989422804014327

AXES = ("x", "ylo", "z", "yhi", "core")
PLANE_Y = ("ylo", "yhi")
f32, bf16 = jnp.float32, jnp.bfloat16


def y_index(y):
    return (y % 2) * 2 + y // 2


def shift(value, axis, by):
    if axis == "y":
        pairs = [(y_index(y), y_index((y + by) % 4)) for y in range(4)]
        return lax.ppermute(value, PLANE_Y, pairs)
    return lax.ppermute(value, axis, [(i, (i + by) % 4) for i in range(4)])


def swap(value):
    return lax.ppermute(value, "core", [(0, 1), (1, 0)])


def ring_gather(own, axis):
    half = own.shape[0] // 2
    left, right = shift(own, axis, 1), shift(own, axis, -1)
    far = jnp.concatenate([shift(left[:half], axis, 1), shift(right[half:], axis, -1)], 0)
    return [own, right, far, left]


def ring_scatter(block, axis):
    far = block(2).astype(bf16)
    half = far.shape[0] // 2
    low, high = shift(far[:half], axis, 1), shift(far[half:], axis, -1)
    ahead, behind = block(1), block(3)
    ahead = jnp.concatenate([ahead[:half] + low.astype(f32), ahead[half:]], 0).astype(bf16)
    behind = jnp.concatenate([behind[:half], behind[half:] + high.astype(f32)], 0).astype(bf16)
    return block(0) + shift(ahead, axis, 1).astype(f32) + shift(behind, axis, -1).astype(f32)


def gelu_parts(pre):
    cdf = 0.5 * (1.0 + lax.erf(pre * ROOT_HALF))
    density = INV_ROOT_TWO_PI * jnp.exp(-0.5 * pre * pre)
    return pre * cdf, cdf + pre * density


def dot(left, right, dims):
    return lax.dot_general(left, right, (dims, ((), ())), preferred_element_type=f32)


def local(inputs, upstream, norm_gain, norm_shift, expand_weight, expand_bias, shrink_weight):
    tokens, width = inputs.shape
    rows, hidden = expand_weight.shape
    half = hidden // 2
    x, ylo, yhi, core = (lax.axis_index(name) for name in ("x", "ylo", "yhi", "core"))
    y = 2 * yhi + ylo

    in_z = lax.all_gather(inputs, "z", axis=0, tiled=True)
    up_z = lax.all_gather(upstream, "z", axis=0, tiled=True)
    in_all = jnp.concatenate([in_z, swap(in_z)], 0)
    up_all = jnp.concatenate([up_z, swap(up_z)], 0)

    def by_core(weight):
        kept = lax.dynamic_slice_in_dim(weight, core * half, half, 1)
        given = swap(lax.dynamic_slice_in_dim(weight, (1 - core) * half, half, 1))
        return jnp.where(core == 0, jnp.concatenate([kept, given], 0), jnp.concatenate([given, kept], 0))

    block_rows = 2 * rows

    def gather_plane(weight, first, second):
        bundle = jnp.stack(ring_gather(by_core(weight), first), 0).reshape(4 * block_rows, half)
        bundles = ring_gather(bundle, second)
        whole = jnp.zeros((width, 2 * half), bf16)
        for far_second in range(4):
            for far_first in range(4):
                piece = bundles[far_second][far_first * block_rows : (far_first + 1) * block_rows]
                if first == "x":
                    px, py = (x + far_first) % 4, (y + far_second) % 4
                else:
                    px, py = (x + far_second) % 4, (y + far_first) % 4
                whole = lax.dynamic_update_slice(whole, piece, ((2 * px + py // 2) * block_rows, (py % 2) * half))
        return whole

    expand_all = gather_plane(expand_weight, "x", "y")
    shrink_all = gather_plane(shrink_weight, "y", "x")
    bias_z = lax.all_gather(expand_bias, "ylo", axis=0, tiled=False)
    bias_own = lax.dynamic_slice_in_dim(bias_z, core * half, half, 1).reshape(2 * half)

    features = in_all.astype(f32)
    centre = jnp.mean(features, axis=1, keepdims=True)
    shifted = features - centre
    scale_inv = lax.rsqrt(jnp.mean(shifted * shifted, axis=1, keepdims=True) + EPSILON)
    normed = shifted * scale_inv
    normed_bf = (normed * norm_gain + norm_shift).astype(bf16)
    pre = dot(normed_bf, expand_all, ((1,), (0,))) + bias_own
    activated, slope = gelu_parts(pre)
    activated = activated.astype(bf16)
    back_act = dot(up_all, shrink_all, ((1,), (0,)))
    back_pre = (back_act * slope).astype(bf16)
    bias_part = jnp.sum(back_pre.astype(f32), axis=0)

    partial_rows = dot(back_pre, expand_all, ((1,), (1,)))
    both = partial_rows[: 4 * tokens] + swap(partial_rows[4 * tokens :].astype(bf16)).astype(f32)
    z = lax.axis_index("z")
    grad_normed = ring_scatter(
        lambda far: lax.dynamic_slice_in_dim(both, ((z + far) % 4) * tokens, tokens, 0), "z"
    )

    def scatter_plane(term, first, second):
        blocks = term.reshape(4, 2, block_rows, 2, half)

        def bundle(far):
            if first == "y":
                py = (y + far) % 4
                got = lax.dynamic_slice(blocks, (0, py // 2, 0, py % 2, 0), (4, 1, block_rows, 1, half))
            else:
                got = lax.dynamic_slice(blocks, ((x + far) % 4, 0, 0, 0, 0), (1, 2, block_rows, 2, half))
                got = got.transpose(0, 1, 3, 2, 4)
            return got.reshape(4 * block_rows, half)

        summed = ring_scatter(bundle, first).reshape(4, block_rows, half)
        here = x if second == "x" else y
        block = ring_scatter(
            lambda far: lax.dynamic_index_in_dim(summed, (here + far) % 4, 0, keepdims=False), second
        )
        kept = lax.dynamic_slice_in_dim(block, core * rows, rows, 0)
        got = swap(lax.dynamic_slice_in_dim(block, (1 - core) * rows, rows, 0))
        return jnp.where(core == 0, jnp.concatenate([kept, got], 1), jnp.concatenate([got, kept], 1))

    shrink_grad = scatter_plane(dot(up_all, activated, ((0,), (0,))), "x", "y")
    expand_grad = scatter_plane(dot(normed_bf, back_pre, ((0,), (0,))), "y", "x")

    own_normed = lax.dynamic_slice_in_dim(normed, z * tokens, tokens, 0)
    own_scale = lax.dynamic_slice_in_dim(scale_inv, z * tokens, tokens, 0)
    weighted = grad_normed * norm_gain
    mean_one = jnp.sum(weighted, axis=1, keepdims=True) / width
    mean_two = jnp.sum(weighted * own_normed, axis=1, keepdims=True) / width
    result = own_scale * (weighted - mean_one - own_normed * mean_two)
    inputs_grad = (upstream.astype(f32) + result).astype(bf16)
    gain_part = jnp.sum(grad_normed * own_normed, axis=0)
    shift_part = jnp.sum(grad_normed, axis=0)
    bias_sum = lax.psum(bias_part, ("x", "ylo", "yhi")).reshape(2, half)
    bias_mine = lax.dynamic_index_in_dim(bias_sum, ylo, 0, keepdims=False)
    bias_other = swap(bias_mine)
    bias_grad = jnp.where(
        core == 0, jnp.concatenate([bias_mine, bias_other]), jnp.concatenate([bias_other, bias_mine])
    )
    gain_grad, shift_grad = lax.psum((gain_part, shift_part), AXES)
    return inputs_grad, gain_grad, shift_grad, expand_grad, bias_grad, shrink_grad


def solution(mesh):
    fine = Mesh(mesh.devices.reshape(4, 2, 4, 2, 2), AXES)
    by_token = P(AXES, None)
    by_weight = P(("x", "yhi", "core"), ("ylo", "z"))
    by_hidden = P(("ylo", "z"))
    return jax.shard_map(
        local,
        mesh=fine,
        in_specs=(by_token, by_token, P(), P(), by_weight, by_hidden, by_weight),
        out_specs=(by_token, P(), P(), by_weight, by_hidden, by_weight),
        check_vma=False,
    )
```

```python
import functools

import jax
import jax.numpy as jnp
from jax import lax
from jax.experimental import pallas as pl
from jax.experimental.pallas import tpu as pltpu
from jax.sharding import Mesh, PartitionSpec as P

EPSILON = 1e-06
ROOT_HALF = 0.7071067811865476
INV_ROOT_TWO_PI = 0.3989422804014327

AXES = ("x", "ylo", "z", "yhi", "core")
PLANE_Y = ("ylo", "yhi")
f32, bf16 = jnp.float32, jnp.bfloat16


def y_index(y):
    return (y % 2) * 2 + y // 2


def shift(value, axis, by):
    if axis == "y":
        pairs = [(y_index(y), y_index((y + by) % 4)) for y in range(4)]
        return lax.ppermute(value, PLANE_Y, pairs)
    return lax.ppermute(value, axis, [(i, (i + by) % 4) for i in range(4)])


def swap(value):
    return lax.ppermute(value, "core", [(0, 1), (1, 0)])


def ring_gather(own, axis):
    half = own.shape[0] // 2
    left, right = shift(own, axis, 1), shift(own, axis, -1)
    return [own, right, shift(left[:half], axis, 1), shift(right[half:], axis, -1), left]


def ring_sum(value, axis):
    return (value + shift(value, axis, 2)) + (shift(value, axis, 1) + shift(value, axis, -1))


def assemble_kernel(first, rows, half, own, right, far_low, far_high, left, whole, sems):
    x = lax.axis_index("x")
    y = 2 * lax.axis_index("yhi") + lax.axis_index("ylo")
    copies = []
    for far_second, far_first in ((s, f) for s in range(4) for f in range(4)):
        if far_second == 2:
            bundle, at = (far_low, far_first) if far_first < 2 else (far_high, far_first - 2)
        else:
            bundle, at = {0: own, 1: right, 3: left}[far_second], far_first
        far_x, far_y = (far_first, far_second) if first == "x" else (far_second, far_first)
        px, py = lax.rem(x + far_x, 4), lax.rem(y + far_y, 4)
        row = pl.multiple_of((2 * px + lax.div(py, 2)) * rows, 16)
        column = pl.multiple_of(lax.rem(py, 2) * half, 128)
        copy = pltpu.make_async_copy(
            bundle.at[pl.ds(at * rows, rows), :],
            whole.at[pl.ds(row, rows), pl.ds(column, half)],
            sems.at[4 * far_second + far_first],
        )
        copy.start()
        copies.append(copy)
    for copy in copies:
        copy.wait()


def assemble(first, rows, bundles):
    half = bundles[0].shape[1]
    return pl.pallas_call(
        functools.partial(assemble_kernel, first, rows, half),
        out_shape=jax.ShapeDtypeStruct((8 * rows, 2 * half), bf16),
        in_specs=[pl.BlockSpec(memory_space=pl.ANY)] * 5,
        out_specs=pl.BlockSpec(memory_space=pl.ANY),
        scratch_shapes=[pltpu.SemaphoreType.DMA((16,))],
        cost_estimate=pl.CostEstimate(flops=0, bytes_accessed=32 * rows * half * 2, transcendentals=0),
    )(*bundles)


def ring_scatter(block, axis):
    far = block(2).astype(bf16)
    half = far.shape[0] // 2
    low, high = shift(far[:half], axis, 1), shift(far[half:], axis, -1)
    ahead, behind = block(1), block(3)
    ahead = jnp.concatenate([ahead[:half] + low.astype(f32), ahead[half:]], 0).astype(bf16)
    behind = jnp.concatenate([behind[:half], behind[half:] + high.astype(f32)], 0).astype(bf16)
    return block(0) + shift(ahead, axis, 1).astype(f32) + shift(behind, axis, -1).astype(f32)


def gelu_parts(pre):
    cdf = 0.5 * (1.0 + lax.erf(pre * ROOT_HALF))
    density = INV_ROOT_TWO_PI * jnp.exp(-0.5 * pre * pre)
    return pre * cdf, cdf + pre * density


def dot(left, right, dims):
    return lax.dot_general(left, right, (dims, ((), ())), preferred_element_type=f32)


def local(inputs, upstream, norm_gain, norm_shift, expand_weight, expand_bias, shrink_weight):
    tokens, width = inputs.shape
    rows, hidden = expand_weight.shape
    half = hidden // 2
    x, ylo, yhi, core = (lax.axis_index(name) for name in ("x", "ylo", "yhi", "core"))
    y = 2 * yhi + ylo

    in_z = lax.all_gather(inputs, "z", axis=0, tiled=True)
    up_z = lax.all_gather(upstream, "z", axis=0, tiled=True)
    in_all = jnp.concatenate([in_z, swap(in_z)], 0)
    up_all = jnp.concatenate([up_z, swap(up_z)], 0)

    def by_core(weight):
        kept = lax.dynamic_slice_in_dim(weight, core * half, half, 1)
        given = swap(lax.dynamic_slice_in_dim(weight, (1 - core) * half, half, 1))
        return jnp.where(core == 0, jnp.concatenate([kept, given], 0), jnp.concatenate([given, kept], 0))

    block_rows = 2 * rows

    def gather_plane(weight, first, second):
        blocks = ring_gather(by_core(weight), first)
        bundle = jnp.concatenate([blocks[0], blocks[1], blocks[2], blocks[3], blocks[4]], 0)
        return assemble(first, block_rows, ring_gather(bundle, second))

    expand_all = gather_plane(expand_weight, "x", "y")
    shrink_all = gather_plane(shrink_weight, "y", "x")
    bias_near = lax.ppermute(expand_bias, "ylo", [(0, 1), (1, 0)])
    bias_both = jnp.where(ylo == 0, jnp.stack([expand_bias, bias_near]), jnp.stack([bias_near, expand_bias]))
    bias_own = lax.dynamic_slice_in_dim(bias_both, core * half, half, 1).reshape(2 * half)

    features = in_all.astype(f32)
    centre = jnp.mean(features, axis=1, keepdims=True)
    shifted = features - centre
    scale_inv = lax.rsqrt(jnp.mean(shifted * shifted, axis=1, keepdims=True) + EPSILON)
    normed = shifted * scale_inv
    normed_bf = (normed * norm_gain + norm_shift).astype(bf16)
    pre = dot(normed_bf, expand_all, ((1,), (0,))) + bias_own
    activated, slope = gelu_parts(pre)
    activated = activated.astype(bf16)
    back_act = dot(up_all, shrink_all, ((1,), (0,)))
    back_pre = (back_act * slope).astype(bf16)
    bias_part = jnp.sum(back_pre.astype(f32), axis=0)

    partial_rows = dot(back_pre, expand_all, ((1,), (1,)))
    both = partial_rows[: 4 * tokens] + swap(partial_rows[4 * tokens :].astype(bf16)).astype(f32)
    z = lax.axis_index("z")
    grad_normed = ring_scatter(
        lambda far: lax.dynamic_slice_in_dim(both, ((z + far) % 4) * tokens, tokens, 0), "z"
    )

    def scatter_plane(term, first, second):
        groups = term.reshape(4, 2 * block_rows, 2 * half)

        def bundle(far):
            if first == "y":
                py = (y + far) % 4
                got = lax.dynamic_slice(groups, (0, py // 2 * block_rows, py % 2 * half), (4, block_rows, half))
                return got.reshape(4 * block_rows, half)
            return lax.dynamic_index_in_dim(groups, (x + far) % 4, 0, keepdims=False)

        summed = ring_scatter(bundle, first)

        def block_of(far):
            if first == "y":
                return lax.dynamic_slice_in_dim(summed, (x + far) % 4 * block_rows, block_rows, 0)
            py = (y + far) % 4
            return lax.dynamic_slice(summed, (py // 2 * block_rows, py % 2 * half), (block_rows, half))

        block = ring_scatter(block_of, second)
        kept = lax.dynamic_slice_in_dim(block, core * rows, rows, 0)
        got = swap(lax.dynamic_slice_in_dim(block, (1 - core) * rows, rows, 0))
        return jnp.where(core == 0, jnp.concatenate([kept, got], 1), jnp.concatenate([got, kept], 1))

    shrink_grad = scatter_plane(dot(up_all, activated, ((0,), (0,))), "x", "y")
    expand_grad = scatter_plane(dot(normed_bf, back_pre, ((0,), (0,))), "y", "x")

    own_normed = lax.dynamic_slice_in_dim(normed, z * tokens, tokens, 0)
    own_scale = lax.dynamic_slice_in_dim(scale_inv, z * tokens, tokens, 0)
    weighted = grad_normed * norm_gain
    mean_one = jnp.sum(weighted, axis=1, keepdims=True) / width
    mean_two = jnp.sum(weighted * own_normed, axis=1, keepdims=True) / width
    result = own_scale * (weighted - mean_one - own_normed * mean_two)
    inputs_grad = (upstream.astype(f32) + result).astype(bf16)
    gain_part = jnp.sum(grad_normed * own_normed, axis=0)
    shift_part = jnp.sum(grad_normed, axis=0)
    norm_part = jnp.concatenate([gain_part, shift_part])
    norm_part = ring_sum(norm_part + swap(norm_part), "z")
    sums = ring_sum(ring_sum(jnp.concatenate([bias_part, norm_part]), "x"), "y")
    gain_grad, shift_grad = sums[2 * half : 2 * half + width], sums[2 * half + width :]
    bias_mine = lax.dynamic_slice_in_dim(sums, ylo * half, half, 0)
    bias_other = swap(bias_mine)
    bias_grad = jnp.where(
        core == 0, jnp.concatenate([bias_mine, bias_other]), jnp.concatenate([bias_other, bias_mine])
    )
    return inputs_grad, gain_grad, shift_grad, expand_grad, bias_grad, shrink_grad


def solution(mesh):
    fine = Mesh(mesh.devices.reshape(4, 2, 4, 2, 2), AXES)
    by_token = P(AXES, None)
    by_weight = P(("x", "yhi", "core"), ("ylo", "z"))
    by_hidden = P(("ylo", "z"))
    return jax.shard_map(
        local,
        mesh=fine,
        in_specs=(by_token, by_token, P(), P(), by_weight, by_hidden, by_weight),
        out_specs=(by_token, P(), P(), by_weight, by_hidden, by_weight),
        check_vma=False,
    )
```

```python
import functools

import jax
import jax.numpy as jnp
from jax import lax
from jax.experimental import pallas as pl
from jax.experimental.pallas import tpu as pltpu
from jax.sharding import Mesh, PartitionSpec as P

EPSILON = 1e-06
ROOT_HALF = 0.7071067811865476
INV_ROOT_TWO_PI = 0.3989422804014327

AXES = ("x", "ylo", "z", "yhi", "core")
PLANE_Y = ("ylo", "yhi")
f32, bf16 = jnp.float32, jnp.bfloat16


def y_index(y):
    return (y % 2) * 2 + y // 2


def shift(value, axis, by):
    if axis == "y":
        pairs = [(y_index(y), y_index((y + by) % 4)) for y in range(4)]
        return lax.ppermute(value, PLANE_Y, pairs)
    return lax.ppermute(value, axis, [(i, (i + by) % 4) for i in range(4)])


def swap(value):
    return lax.ppermute(value, "core", [(0, 1), (1, 0)])


def after(value, *others):
    return lax.optimization_barrier((value, *others))[0]


def direct_gather(own, axis):
    return [own, shift(own, axis, -1), shift(own, axis, 2), shift(own, axis, 1)]


def ring_gather(own, axis):
    half = own.shape[0] // 2
    left, right = shift(own, axis, 1), shift(own, axis, -1)
    low, high = left[:half], right[half:]
    return [own, right, shift(low, axis, 1), shift(high, axis, -1), left], (low, high)


def ring_scatter(block, far, axis):
    half = far[0].shape[0]
    low, high = shift(far[0], axis, 1), shift(far[1], axis, -1)
    ahead, behind = block(1), block(3)
    ahead = jnp.concatenate([ahead[:half] + low.astype(f32), ahead[half:]], 0).astype(bf16)
    behind = jnp.concatenate([behind[:half], behind[half:] + high.astype(f32)], 0).astype(bf16)
    return block(0) + shift(ahead, axis, 1).astype(f32) + shift(behind, axis, -1).astype(f32)


def parts_of(value, rows, columns):
    high = lax.reduce_precision(value, 8, 7)
    low = lax.reduce_precision(value - high, 8, 7)
    flat = jnp.concatenate([high, low])
    return jnp.pad(flat, (0, rows * columns - flat.size)).reshape(rows, columns).astype(bf16)


def from_parts(rows, size):
    flat = rows.astype(f32).reshape(-1)
    return flat[:size] + flat[size : 2 * size]


def direct_scatter(block, vector, rider, axis):
    rows, columns = block(0).shape
    riding = parts_of(vector, rider, columns)
    got = [shift(jnp.concatenate([block(by).astype(bf16), riding], 0), axis, by) for by in (1, 2, 3)]
    ahead, far, behind = (part[:rows].astype(f32) for part in got)
    own, v_ahead, v_far, v_behind = (from_parts(part, vector.size) for part in (riding, *(p[rows:] for p in got)))
    return block(0) + ahead + behind + far, (own + v_far) + (v_ahead + v_behind)


def assemble_kernel(first, rows, half, own, right, far_low, far_high, left, whole, sems):
    x = lax.axis_index("x")
    y = 2 * lax.axis_index("yhi") + lax.axis_index("ylo")
    copies = []
    for far_second, far_first in ((s, f) for s in range(4) for f in range(4)):
        if far_second == 2:
            bundle, at = (far_low, far_first) if far_first < 2 else (far_high, far_first - 2)
        else:
            bundle, at = {0: own, 1: right, 3: left}[far_second], far_first
        far_x, far_y = (far_first, far_second) if first == "x" else (far_second, far_first)
        px, py = lax.rem(x + far_x, 4), lax.rem(y + far_y, 4)
        row = pl.multiple_of((2 * px + lax.div(py, 2)) * rows, 16)
        column = pl.multiple_of(lax.rem(py, 2) * half, 128)
        copy = pltpu.make_async_copy(
            bundle.at[pl.ds(at * rows, rows), :],
            whole.at[pl.ds(row, rows), pl.ds(column, half)],
            sems.at[4 * far_second + far_first],
        )
        copy.start()
        copies.append(copy)
    for copy in copies:
        copy.wait()


def assemble(first, rows, bundles):
    half = bundles[0].shape[1]
    return pl.pallas_call(
        functools.partial(assemble_kernel, first, rows, half),
        out_shape=jax.ShapeDtypeStruct((8 * rows, 2 * half), bf16),
        in_specs=[pl.BlockSpec(memory_space=pl.ANY)] * 5,
        out_specs=pl.BlockSpec(memory_space=pltpu.VMEM),
        scratch_shapes=[pltpu.SemaphoreType.DMA((16,))],
        compiler_params=pltpu.CompilerParams(vmem_limit_bytes=16 * 2**20),
        cost_estimate=pl.CostEstimate(flops=0, bytes_accessed=32 * rows * half * 2, transcendentals=0),
    )(*bundles)


def gelu_parts(pre):
    cdf = 0.5 * (1.0 + lax.erf(pre * ROOT_HALF))
    density = INV_ROOT_TWO_PI * jnp.exp(-0.5 * pre * pre)
    return pre * cdf, cdf + pre * density


def dot(left, right, dims):
    return lax.dot_general(left, right, (dims, ((), ())), preferred_element_type=f32)


def local(inputs, upstream, norm_gain, norm_shift, expand_weight, expand_bias, shrink_weight):
    tokens, width = inputs.shape
    rows, hidden = expand_weight.shape
    half = hidden // 2
    x, ylo, z, yhi, core = (lax.axis_index(name) for name in AXES)
    y = 2 * yhi + ylo

    def by_core(weight):
        kept = lax.dynamic_slice_in_dim(weight, core * half, half, 1)
        given = swap(lax.dynamic_slice_in_dim(weight, (1 - core) * half, half, 1))
        return jnp.where(core == 0, jnp.concatenate([kept, given], 0), jnp.concatenate([given, kept], 0))

    block_rows = 2 * rows

    def gather_plane(weight, first, second):
        bundle = jnp.concatenate(direct_gather(by_core(weight), first), 0)
        return ring_gather(bundle, second)

    in_near = lax.all_gather(inputs, "z", axis=0, tiled=True)
    up_near, _ = ring_gather(upstream, "z")
    up_near = jnp.concatenate(up_near, 0)
    expand_blocks, expand_sent = gather_plane(expand_weight, "x", "y")
    shrink_blocks, shrink_sent = gather_plane(shrink_weight, "y", "x")
    up_near = after(up_near, expand_sent, shrink_sent)
    in_near = after(in_near, expand_sent, shrink_sent)
    up_all = jnp.concatenate([up_near, swap(up_near)], 0)

    def by_distance(value):
        return lax.dynamic_slice_in_dim(jnp.concatenate([value, value], 0), z * tokens, 4 * tokens, 0)

    in_all = jnp.concatenate([by_distance(in_near), by_distance(swap(in_near))], 0)
    expand_all = assemble("x", block_rows, expand_blocks)
    shrink_all = assemble("y", block_rows, shrink_blocks)
    bias_near = lax.ppermute(expand_bias, "ylo", [(0, 1), (1, 0)])
    bias_both = jnp.where(ylo == 0, jnp.stack([expand_bias, bias_near]), jnp.stack([bias_near, expand_bias]))
    bias_own = lax.dynamic_slice_in_dim(bias_both, core * half, half, 1).reshape(2 * half)

    features = in_all.astype(f32)
    centre = jnp.mean(features, axis=1, keepdims=True)
    shifted = features - centre
    scale_inv = lax.rsqrt(jnp.mean(shifted * shifted, axis=1, keepdims=True) + EPSILON)
    normed = shifted * scale_inv
    normed_bf = lax.optimization_barrier((normed * norm_gain + norm_shift).astype(bf16))
    pre = dot(normed_bf, expand_all, ((1,), (0,))) + bias_own
    activated, slope = gelu_parts(pre)
    activated = activated.astype(bf16)
    def groups_of(term):
        return term.reshape(4, 2 * block_rows, 2 * half)

    def shrink_bundle(far):
        return lax.dynamic_index_in_dim(shrink_term, (x + far) % 4, 0, keepdims=False)

    def expand_bundle(far):
        py = (y + far) % 4
        got = lax.dynamic_slice(expand_term, (0, py // 2 * block_rows, py % 2 * half), (4, block_rows, half))
        return got.reshape(4 * block_rows, half)

    def halves(bundle):
        rows = bundle.shape[0] // 2
        return lax.optimization_barrier((bundle[:rows].astype(bf16), bundle[rows:].astype(bf16)))

    shrink_term = groups_of(dot(up_all, activated, ((0,), (0,))))
    shrink_far = halves(shrink_bundle(2))
    back_act = dot(after(up_all, shrink_far), shrink_all, ((1,), (0,)))
    back_pre = (back_act * slope).astype(bf16)
    bias_part = jnp.sum(back_pre.astype(f32), axis=0)
    expand_term = groups_of(dot(normed_bf, back_pre, ((0,), (0,))))
    expand_far = halves(expand_bundle(2))
    shrink_sum = ring_scatter(shrink_bundle, shrink_far, "x")
    expand_sum = ring_scatter(expand_bundle, expand_far, "y")

    partial_rows = dot(after(back_pre, expand_far), expand_all, ((1,), (1,)))
    norm_part = jnp.concatenate([jnp.sum(partial_rows * normed, axis=0), jnp.sum(partial_rows, axis=0)])
    both = partial_rows[: 4 * tokens] + swap(partial_rows[4 * tokens :].astype(bf16)).astype(f32)
    norm_part = norm_part + swap(norm_part)
    grad_normed, norm_part = direct_scatter(
        lambda far: both[far * tokens : (far + 1) * tokens], norm_part, 16, "z"
    )

    def shrink_block(far):
        py = (y + far) % 4
        return lax.dynamic_slice(shrink_sum, (py // 2 * block_rows, py % 2 * half), (block_rows, half))

    def expand_block(far):
        return lax.dynamic_slice_in_dim(expand_sum, (x + far) % 4 * block_rows, block_rows, 0)

    sums = jnp.concatenate([bias_part, norm_part])
    shrink_own, sums = direct_scatter(shrink_block, sums, 32, "y")
    expand_own, sums = direct_scatter(expand_block, sums, 32, "x")

    def by_rows(block):
        kept = lax.dynamic_slice_in_dim(block, core * rows, rows, 0)
        got = swap(lax.dynamic_slice_in_dim(block, (1 - core) * rows, rows, 0))
        return jnp.where(core == 0, jnp.concatenate([kept, got], 1), jnp.concatenate([got, kept], 1))

    shrink_grad, expand_grad = by_rows(shrink_own), by_rows(expand_own)
    bias_mine = lax.dynamic_slice_in_dim(sums, ylo * half, half, 0)
    bias_other = swap(bias_mine)
    bias_grad = jnp.where(
        core == 0, jnp.concatenate([bias_mine, bias_other]), jnp.concatenate([bias_other, bias_mine])
    )
    gain_grad, shift_grad = sums[2 * half : 2 * half + width], sums[2 * half + width :]

    own_normed, own_scale = normed[:tokens], scale_inv[:tokens]
    weighted = grad_normed * norm_gain
    mean_one = jnp.sum(weighted, axis=1, keepdims=True) / width
    mean_two = jnp.sum(weighted * own_normed, axis=1, keepdims=True) / width
    result = own_scale * (weighted - mean_one - own_normed * mean_two)
    inputs_grad = (upstream.astype(f32) + result).astype(bf16)
    return inputs_grad, gain_grad, shift_grad, expand_grad, bias_grad, shrink_grad


def solution(mesh):
    fine = Mesh(mesh.devices.reshape(4, 2, 4, 2, 2), AXES)
    by_token = P(AXES, None)
    by_weight = P(("x", "yhi", "core"), ("ylo", "z"))
    by_hidden = P(("ylo", "z"))
    return jax.shard_map(
        local,
        mesh=fine,
        in_specs=(by_token, by_token, P(), P(), by_weight, by_hidden, by_weight),
        out_specs=(by_token, P(), P(), by_weight, by_hidden, by_weight),
        check_vma=False,
    )
```

```python
import functools

import jax
import jax.numpy as jnp
from jax import lax
from jax.experimental import pallas as pl
from jax.experimental.pallas import tpu as pltpu
from jax.sharding import Mesh, PartitionSpec as P

EPSILON = 1e-06
ROOT_HALF = 0.7071067811865476
INV_ROOT_TWO_PI = 0.3989422804014327

AXES = ("x", "ylo", "z", "yhi", "core")
PLANE_Y = ("ylo", "yhi")
f32, bf16 = jnp.float32, jnp.bfloat16


def y_index(y):
    return (y % 2) * 2 + y // 2


def shift(value, axis, by):
    if axis == "y":
        pairs = [(y_index(y), y_index((y + by) % 4)) for y in range(4)]
        return lax.ppermute(value, PLANE_Y, pairs)
    return lax.ppermute(value, axis, [(i, (i + by) % 4) for i in range(4)])


def swap(value):
    return lax.ppermute(value, "core", [(0, 1), (1, 0)])


def after(value, *others):
    return lax.optimization_barrier((value, *others))[0]


def both_ways(ahead, behind, axis):
    return shift(ahead, axis, 1), shift(behind, axis, -1)


def ring_sum(value, axis):
    return (value + shift(value, axis, 2)) + (shift(value, axis, 1) + shift(value, axis, -1))


def parts_of(vector):
    high = lax.reduce_precision(vector, 8, 7)
    return jnp.concatenate([high, lax.reduce_precision(vector - high, 8, 7)], 0).astype(bf16)


def from_parts(rows):
    return rows[:16].astype(f32) + rows[16:].astype(f32)


def direct_scatter(block, axis, vector=None):
    rows = block(0).shape[0]
    riding = [] if vector is None else [parts_of(vector)]
    got = [shift(jnp.concatenate([block(by).astype(bf16), *riding], 0), axis, by) for by in (1, 2, 3)]
    ahead, far, behind = (part[:rows].astype(f32) for part in got)
    summed = block(0) + ahead + behind + far
    if vector is None:
        return summed, None
    own, v_ahead, v_far, v_behind = (from_parts(part) for part in (*riding, *(p[rows:] for p in got)))
    return summed, (own + v_far) + (v_ahead + v_behind)


def assemble_kernel(first, own, right, far_low, far_high, left, whole):
    x, y = place()
    rows, half = own.shape[0] // 4, own.shape[1]
    for far_second in range(4):
        for far_first in range(4):
            if far_second == 2:
                bundle, at = (far_low, far_first) if far_first < 2 else (far_high, far_first - 2)
            else:
                bundle, at = {0: own, 1: right, 3: left}[far_second], far_first
            far_x, far_y = (far_first, far_second) if first == "x" else (far_second, far_first)
            px, py = lax.rem(x + far_x, 4), lax.rem(y + far_y, 4)
            row = pl.multiple_of((2 * px + lax.div(py, 2)) * rows, 16)
            column = pl.multiple_of(lax.rem(py, 2) * half, 128)
            whole[pl.ds(row, rows), pl.ds(column, half)] = bundle[at * rows : (at + 1) * rows, :]


def place():
    return lax.axis_index("x"), 2 * lax.axis_index("yhi") + lax.axis_index("ylo")


def gelu_parts(pre):
    cdf = 0.5 * (1.0 + lax.erf(pre * ROOT_HALF))
    density = INV_ROOT_TWO_PI * jnp.exp(-0.5 * pre * pre)
    return pre * cdf, cdf + pre * density


def dot(left, right, dims=((1,), (0,))):
    return lax.dot_general(left, right, (dims, ((), ())), preferred_element_type=f32)


def call(kernel, outs, args, scratch=(), aliases=None, limit=16):
    return pl.pallas_call(
        kernel,
        out_shape=[jax.ShapeDtypeStruct(shape, dtype) for shape, dtype in outs],
        in_specs=[pl.BlockSpec(memory_space=pltpu.VMEM)] * len(args),
        out_specs=[pl.BlockSpec(memory_space=pltpu.VMEM)] * len(outs),
        scratch_shapes=list(scratch),
        input_output_aliases=aliases or {},
        compiler_params=pltpu.CompilerParams(vmem_limit_bytes=limit * 2**20),
        cost_estimate=pl.CostEstimate(flops=10**6, bytes_accessed=10**6, transcendentals=0),
    )(*args)


def norm_kernel(half, part, gain, shift_by, *refs):
    normed, centre, scale, normed_t, up_t, turned = refs[-6:]
    tokens, width = part.shape[2:]
    to, rows = pl.ds(half * 4 * tokens, 4 * tokens), width // 8

    def normalise(k, _):
        at = pl.ds(pl.multiple_of(k * tokens, 16), tokens)
        features = part[k, 0].astype(f32)
        mean = jnp.mean(features, axis=1, keepdims=True)
        shifted = features - mean
        inv = lax.rsqrt(jnp.mean(shifted * shifted, axis=1, keepdims=True) + EPSILON)
        normed[at, :] = (shifted * inv * gain[...] + shift_by[...]).astype(bf16)
        centre[at, :] = mean
        scale[at, :] = inv
        return 0

    def turn(c, _):
        lanes = pl.ds(pl.multiple_of(c * 128, 128), 128)
        up_t[lanes, to] = jnp.concatenate([part[k, 1, :, lanes] for k in range(4)], 0).T
        turned[lanes, :] = normed[:, lanes].T
        return 0

    def order(b, _):
        at = pl.multiple_of((lax.rem(b, 2) * 4 + lax.div(b, 2)) * rows, 16)
        normed_t[pl.ds(at, rows), to] = turned[pl.ds(pl.multiple_of(b * rows, 16), rows), :]
        return 0

    lax.fori_loop(0, 4, normalise, 0)
    lax.fori_loop(0, width // 128, turn, 0)
    lax.fori_loop(0, 8, order, 0)


def hidden_kernel(half, part, normed, expand, shrink, bias, *refs):
    bias_sum, active, back, pre_tile, back_tile = refs[-5:]
    tokens, width = part.shape[2:]
    tile, to = 256, pl.ds(half * 4 * tokens, 4 * tokens)
    tiles = expand.shape[1] // tile

    def lanes_of(j):
        return pl.ds(pl.multiple_of(j * tile, tile), tile)

    def products(j, slot):
        lanes = lanes_of(j)
        pre_tile[slot] = dot(normed[...], expand[:, lanes])
        back_tile[slot] = dot(jnp.concatenate([part[k, 1] for k in range(4)], 0), shrink[:, lanes])

    def finish(j, slot):
        lanes = lanes_of(j)
        value, slope = gelu_parts(pre_tile[slot] + bias[:, lanes])
        active[to, lanes] = value.astype(bf16)
        grad = (back_tile[slot] * slope).astype(bf16)
        back[to, lanes] = grad
        bias_sum[:, lanes] = jnp.sum(grad.astype(f32), axis=0, keepdims=True)

    def step(j, _):
        products(2 * j + 1, 1)
        finish(2 * j, 0)
        following = lax.rem(2 * j + 2, tiles)
        products(following, 0)
        finish(2 * j + 1, 1)
        return 0

    products(0, 0)
    lax.fori_loop(0, tiles // 2, step, 0)


def shrink_tile(far, n, up_t, active):
    x, _ = place()
    rows, lanes = up_t.shape[0] // 4, pl.ds(pl.multiple_of(n * 256, 256), 256)
    return lanes, dot(up_t[pl.ds(pl.multiple_of(lax.rem(x + far, 4) * rows, 16), rows), :], active[:, lanes])


def expand_tile(far, n, normed_t, back):
    _, y = place()
    py = lax.rem(y + far, 4)
    rows, half = normed_t.shape[0] // 2, back.shape[1] // 2
    right = back[:, pl.ds(pl.multiple_of(lax.rem(py, 2) * half + n * 256, 256), 256)]
    left = normed_t[pl.ds(pl.multiple_of(lax.div(py, 2) * rows, 16), rows), :]
    return pl.ds(pl.multiple_of(n * 256, 256), 256), dot(left, right)


def far_kernel(up_t, active, normed_t, back, sums, bias, shrink_low, shrink_high, expand_low, expand_high, vector):
    def tile_of(make, left, right, low, high):
        def step(n, _):
            lanes, term = make(2, n, left, right)
            rows = term.shape[0] // 2
            low[pl.ds(0, rows), lanes] = term[:rows].astype(bf16)
            high[pl.ds(0, rows), lanes] = term[rows:].astype(bf16)
            return 0

        return step

    lax.fori_loop(0, active.shape[1] // 256, tile_of(shrink_tile, up_t, active, shrink_low, shrink_high), 0)
    lax.fori_loop(0, back.shape[1] // 512, tile_of(expand_tile, normed_t, back, expand_low, expand_high), 0)
    half, width = expand_low.shape[1], sums.shape[1]
    vector[...] = jnp.zeros_like(vector)
    for i in range(2):
        for j, start in enumerate(range(0, width, half)):
            size = min(half, width - start)
            vector[4 * i + j : 4 * i + j + 1, :size] = sums[i : i + 1, start : start + size]
        vector[8 + i : 9 + i, :] = bias[:, i * half : (i + 1) * half]
    high = vector[...].astype(bf16)
    riding = jnp.concatenate([high, (vector[...] - high.astype(f32)).astype(bf16)], 0)
    for to in (expand_low, expand_high):
        to[to.shape[0] - 32 :, :] = riding
    vector[...] = riding[:16].astype(f32) + riding[16:].astype(f32)


def near_kernel(up_t, active, normed_t, back, shrink_own, expand_own, shrink_terms, expand_terms):
    def tile_of(make, left, right, own, terms):
        def for_own(n, _):
            lanes, term = make(0, n, left, right)
            own[:, lanes] = term
            return 0

        def for_others(i, _):
            d, n = lax.rem(i, 2), lax.div(i, 2)
            lanes, term = make(1 + 2 * d, n, left, right)
            terms[d, :, lanes] = term
            return 0

        return for_own, for_others

    for make, left, right, own, terms in (
        (shrink_tile, up_t, active, shrink_own, shrink_terms),
        (expand_tile, normed_t, back, expand_own, expand_terms),
    ):
        tiles = own.shape[1] // 256
        for_own, for_others = tile_of(make, left, right, own, terms)
        lax.fori_loop(0, 2 * tiles, for_others, 0)
        lax.fori_loop(0, tiles, for_own, 0)


def pass_kernel(s_terms, e_terms, s_low, s_high, e_low, e_high, s_ahead, s_behind, e_ahead, e_behind):
    for terms, low, high, ahead, behind in (
        (s_terms, s_low, s_high, s_ahead, s_behind),
        (e_terms, e_low, e_high, e_ahead, e_behind),
    ):
        rows = terms.shape[1] // 2

        def step(i, _, rows=rows, terms=terms, low=low, high=high, ahead=ahead, behind=behind):
            at, then = pl.ds(pl.multiple_of(i * 16, 16), 16), pl.ds(pl.multiple_of(rows + i * 16, 16), 16)
            ahead[at, :] = (terms[0, at, :] + low[at, :].astype(f32)).astype(bf16)
            ahead[then, :] = terms[0, then, :].astype(bf16)
            behind[at, :] = terms[1, at, :].astype(bf16)
            behind[then, :] = (terms[1, then, :] + high[at, :].astype(f32)).astype(bf16)
            return 0

        lax.fori_loop(0, rows // 16, step, 0)
    rows = e_terms.shape[1]
    e_ahead[rows:, :] = e_low[rows // 2 :, :]


def rows_kernel(near, other, near_centre, other_centre, near_scale, other_scale, back, expand, mine, others, sums):
    tokens, width = near.shape[2:]

    def tile_of(lanes):
        gain = plain = 0.0
        for half, part, centre, scale in ((1, other, other_centre, other_scale), (0, near, near_centre, near_scale)):
            rows = dot(back[pl.ds(half * 4 * tokens, 4 * tokens), :], expand[lanes, :], ((1,), (1,)))
            features = jnp.concatenate([part[k, 0, :, lanes] for k in range(4)], 0).astype(f32)
            normed = (features - centre[...]) * scale[...]
            gain = gain + jnp.sum(rows * normed, axis=0, keepdims=True)
            plain = plain + jnp.sum(rows, axis=0, keepdims=True)
            if half:
                others[:, lanes] = rows.astype(bf16)
            else:
                mine[:, lanes] = rows
        sums[0:1, lanes] = gain
        sums[1:2, lanes] = plain

    def step(j, _):
        tile_of(pl.ds(pl.multiple_of(j * 256, 256), 256))
        return 0

    whole = width // 256
    lax.fori_loop(0, whole, step, 0)
    if width % 256:
        tile_of(slice(whole * 256, width))


def local(inputs, upstream, norm_gain, norm_shift, expand_weight, expand_bias, shrink_weight):
    tokens, width = inputs.shape
    rows, hidden = expand_weight.shape
    half = hidden // 2
    x, ylo, z, yhi, core = (lax.axis_index(name) for name in AXES)
    y = 2 * yhi + ylo

    def by_core(weight):
        kept = lax.dynamic_slice_in_dim(weight, core * half, half, 1)
        given = swap(lax.dynamic_slice_in_dim(weight, (1 - core) * half, half, 1))
        return jnp.where(core == 0, jnp.concatenate([kept, given], 0), jnp.concatenate([given, kept], 0))

    block_rows = 2 * rows

    bias_near = lax.ppermute(expand_bias, "ylo", [(0, 1), (1, 0)])
    a, b, bias_near = lax.optimization_barrier((by_core(expand_weight), by_core(shrink_weight), bias_near))

    near = lax.all_gather(jnp.stack([inputs, upstream])[None], "z", axis=0, tiled=True)

    (a_left, a_right), (b_left, b_right) = both_ways(a, a, "x"), both_ways(b, b, "y")
    a_low, a_high = both_ways(a_left[:rows], a_right[rows:], "x")
    b_low, b_high = both_ways(b_left[:rows], b_right[rows:], "y")
    a = jnp.concatenate([a, a_right, a_low, a_high, a_left], 0)
    b = jnp.concatenate([b, b_right, b_low, b_high, b_left], 0)
    (a_left, a_right), (b_left, b_right) = both_ways(a, a, "y"), both_ways(b, b, "x")
    halves = a_left[: 2 * block_rows], a_right[2 * block_rows :], b_left[: 2 * block_rows], b_right[2 * block_rows :]
    a_low, a_high = both_ways(*halves[:2], "y")
    b_low, b_high = both_ways(*halves[2:], "x")
    weight_shape = [((width, 2 * half), bf16)]
    (expand_all,) = call(functools.partial(assemble_kernel, "x"), weight_shape, (a, a_right, a_low, a_high, a_left))
    (shrink_all,) = call(functools.partial(assemble_kernel, "y"), weight_shape, (b, b_right, b_low, b_high, b_left))
    bias_both = jnp.where(ylo == 0, jnp.stack([expand_bias, bias_near]), jnp.stack([bias_near, expand_bias]))
    bias_own = lax.dynamic_slice_in_dim(bias_both, core * half, half, 1).reshape(1, 2 * half)

    near = after(near, a_low, a_high, b_low, b_high)
    other = swap(near)
    many = 8 * tokens
    tall, wide = ((width, many), bf16), ((many, 2 * half), bf16)
    column, own_normed_shape = ((4 * tokens, 1), f32), ((4 * tokens, width), bf16)
    gain, shift_by = norm_gain[None], norm_shift[None]

    def normalise(which, part, *so_far):
        return call(
            functools.partial(norm_kernel, which),
            [own_normed_shape, column, column, tall, tall],
            (part, gain, shift_by, *so_far),
            scratch=[pltpu.VMEM((width, 4 * tokens), bf16)],
            aliases={3: 3, 4: 4} if so_far else None,
        )

    def project(which, part, normed, *so_far):
        tiles = pltpu.VMEM((2, 4 * tokens, 256), f32)
        return call(
            functools.partial(hidden_kernel, which),
            [((1, 2 * half), f32), wide, wide],
            (part, normed, expand_all, shrink_all, bias_own, *so_far),
            scratch=[tiles, tiles],
            aliases={5: 1, 6: 2} if so_far else None,
        )

    normed, near_centre, near_scale, *turned = normalise(0, near)
    near_bias, *hidden_parts = project(0, near, normed)
    normed, other_centre, other_scale, normed_t, up_t = normalise(1, other, *turned)
    other_bias, active, back = project(1, other, normed, *hidden_parts)
    bias_part = near_bias + other_bias

    mine, others, norm_sums = call(
        rows_kernel,
        [((4 * tokens, width), f32), ((4 * tokens, width), bf16), ((2, width), f32)],
        (near, other, near_centre, other_centre, near_scale, other_scale, back, expand_all),
    )

    short, long = ((block_rows, 2 * half), bf16), ((2 * block_rows + 32, half), bf16)
    s_low, s_high, e_low, e_high, vector = call(
        far_kernel,
        [short, short, long, long, ((16, half), f32)],
        (up_t, active, normed_t, back, norm_sums, bias_part),
    )
    (s_low, s_high), (e_low, e_high), sent = both_ways(s_low, s_high, "x"), both_ways(e_low, e_high, "y"), s_low
    s_wide, e_wide = (2 * block_rows, 2 * half), (4 * block_rows, half)
    s_own, e_own, s_terms, e_terms = call(
        near_kernel,
        [(s_wide, f32), (e_wide, f32), ((2, *s_wide), f32), ((2, *e_wide), f32)],
        (up_t, active, normed_t, after(back, sent)),
    )
    s_ahead, s_behind, e_ahead, e_behind = call(
        pass_kernel,
        [(s_wide, bf16), (s_wide, bf16), ((4 * block_rows + 32, half), bf16), (e_wide, bf16)],
        (s_terms, e_terms, s_low, s_high, e_low, e_high),
    )
    (s_prev, s_next), (e_prev, e_next) = both_ways(s_ahead, s_behind, "x"), both_ways(e_ahead, e_behind, "y")

    both = after(mine, s_own) + swap(after(others, sent)).astype(f32)
    grad_normed = lax.psum_scatter(both.astype(bf16), "z", scatter_dimension=0, tiled=True).astype(f32)

    s_sum = s_own + s_prev.astype(f32) + s_next.astype(f32)
    e_sum = e_own + e_prev[: 4 * block_rows].astype(f32) + e_next.astype(f32)
    v_prev, v_next, v_far = (
        from_parts(part) for part in (e_low[2 * block_rows :], e_high[2 * block_rows :], e_prev[4 * block_rows :])
    )
    vector = (vector + v_far) + (v_prev + v_next)

    def shrink_block(far):
        py = (y + far) % 4
        return lax.dynamic_slice(s_sum, (py // 2 * block_rows, py % 2 * half), (block_rows, half))

    def expand_block(far):
        return lax.dynamic_slice_in_dim(e_sum, (x + far) % 4 * block_rows, block_rows, 0)

    def by_rows(block):
        kept = lax.dynamic_slice_in_dim(block, core * rows, rows, 0)
        got = swap(lax.dynamic_slice_in_dim(block, (1 - core) * rows, rows, 0))
        return jnp.where(core == 0, jnp.concatenate([kept, got], 1), jnp.concatenate([got, kept], 1))

    expand_own, vector = direct_scatter(expand_block, "x", vector)
    shrink_own, _ = direct_scatter(shrink_block, "y")
    norm_sums = ring_sum(vector[:8], "z")
    norm_sums = norm_sums + swap(norm_sums)
    gain_grad, shift_grad = (norm_sums[i : i + 4].reshape(-1)[:width] for i in (0, 4))
    bias_mine = lax.dynamic_index_in_dim(vector, 8 + ylo, 0, keepdims=False)
    bias_other = swap(bias_mine)
    bias_grad = jnp.where(
        core == 0, jnp.concatenate([bias_mine, bias_other]), jnp.concatenate([bias_other, bias_mine])
    )
    shrink_grad, expand_grad = by_rows(shrink_own), by_rows(expand_own)

    features = inputs.astype(f32)
    own_centre = jnp.mean(features, axis=1, keepdims=True)
    shifted = features - own_centre
    own_scale = lax.rsqrt(jnp.mean(shifted * shifted, axis=1, keepdims=True) + EPSILON)
    own_normed = shifted * own_scale
    weighted = grad_normed * norm_gain
    mean_one = jnp.sum(weighted, axis=1, keepdims=True) / width
    mean_two = jnp.sum(weighted * own_normed, axis=1, keepdims=True) / width
    result = own_scale * (weighted - mean_one - own_normed * mean_two)
    inputs_grad = (upstream.astype(f32) + result).astype(bf16)
    return inputs_grad, gain_grad, shift_grad, expand_grad, bias_grad, shrink_grad


def solution(mesh):
    fine = Mesh(mesh.devices.reshape(4, 2, 4, 2, 2), AXES)
    by_token = P(AXES, None)
    by_weight = P(("x", "yhi", "core"), ("ylo", "z"))
    by_hidden = P(("ylo", "z"))
    return jax.shard_map(
        local,
        mesh=fine,
        in_specs=(by_token, by_token, P(), P(), by_weight, by_hidden, by_weight),
        out_specs=(by_token, P(), P(), by_weight, by_hidden, by_weight),
        check_vma=False,
    )
```

```python
import functools

import jax
import jax.numpy as jnp
from jax import lax
from jax.experimental import pallas as pl
from jax.experimental.pallas import tpu as pltpu
from jax.sharding import Mesh, PartitionSpec as P

EPSILON = 1e-06
ROOT_HALF = 0.7071067811865476
INV_ROOT_TWO_PI = 0.3989422804014327

AXES = ("x", "ylo", "z", "yhi", "core")
PLANE_Y = ("ylo", "yhi")
f32, bf16 = jnp.float32, jnp.bfloat16


def y_index(y):
    return (y % 2) * 2 + y // 2


def shift(value, axis, by):
    if axis == "y":
        pairs = [(y_index(y), y_index((y + by) % 4)) for y in range(4)]
        return lax.ppermute(value, PLANE_Y, pairs)
    return lax.ppermute(value, axis, [(i, (i + by) % 4) for i in range(4)])


def swap(value):
    return lax.ppermute(value, "core", [(0, 1), (1, 0)])


def after(value, *others):
    return lax.optimization_barrier((value, *others))[0]


def both_ways(ahead, behind, axis):
    return shift(ahead, axis, 1), shift(behind, axis, -1)


def pair_sum(value, axis):
    for bit in (1, 2):
        value = value + lax.ppermute(value, axis, [(i, i ^ bit) for i in range(4)])
    return value


def from_parts(rows):
    return rows[:16].astype(f32) + rows[16:].astype(f32)


def direct(ahead, far, behind, axis):
    return shift(ahead, axis, 1), shift(far, axis, 2), shift(behind, axis, 3)


def assemble_kernel(first, own, right, far_low, far_high, left, whole):
    x, y = place()
    rows, half = own.shape[0] // 4, own.shape[1]
    for far_second in range(4):
        for far_first in range(4):
            if far_second == 2:
                bundle, at = (far_low, far_first) if far_first < 2 else (far_high, far_first - 2)
            else:
                bundle, at = {0: own, 1: right, 3: left}[far_second], far_first
            far_x, far_y = (far_first, far_second) if first == "x" else (far_second, far_first)
            px, py = lax.rem(x + far_x, 4), lax.rem(y + far_y, 4)
            row = pl.multiple_of((2 * px + lax.div(py, 2)) * rows, 16)
            column = pl.multiple_of(lax.rem(py, 2) * half, 128)
            whole[pl.ds(row, rows), pl.ds(column, half)] = bundle[at * rows : (at + 1) * rows, :]


def place():
    return lax.axis_index("x"), 2 * lax.axis_index("yhi") + lax.axis_index("ylo")


def gelu_parts(pre):
    cdf = 0.5 * (1.0 + lax.erf(pre * ROOT_HALF))
    density = INV_ROOT_TWO_PI * jnp.exp(-0.5 * pre * pre)
    return pre * cdf, cdf + pre * density


def dot(left, right, dims=((1,), (0,))):
    return lax.dot_general(left, right, (dims, ((), ())), preferred_element_type=f32)


def call(kernel, outs, args, scratch=(), aliases=None, behind=(), mark=False, limit=16):
    given, made = len(args), len(outs)

    def body(*refs):
        refs = refs[:given] + refs[given + len(behind) :]
        if mark:
            refs[given + made][...] = jnp.zeros_like(refs[given + made])
            refs = refs[: given + made] + refs[given + made + 1 :]
        kernel(*refs)

    outs = [*outs, *[((8, 128), f32)] * mark]
    whole = pl.BlockSpec(memory_space=pltpu.VMEM)
    return pl.pallas_call(
        body,
        out_shape=[jax.ShapeDtypeStruct(shape, dtype) for shape, dtype in outs],
        in_specs=[whole] * (given + len(behind)),
        out_specs=[whole] * len(outs),
        scratch_shapes=list(scratch),
        input_output_aliases=aliases or {},
        compiler_params=pltpu.CompilerParams(vmem_limit_bytes=limit * 2**20),
        cost_estimate=pl.CostEstimate(flops=10**6, bytes_accessed=10**6, transcendentals=0),
    )(*args, *behind)


def stack_kernel(inputs, upstream, stacked):
    stacked[0, 0] = inputs[...]
    stacked[0, 1] = upstream[...]


def nothing_kernel(*refs):
    pass


def add_kernel(mine, others, total):
    def step(i, _):
        at = pl.ds(pl.multiple_of(i * 32, 32), 32)
        total[at, :] = (mine[at, :] + others[at, :].astype(f32)).astype(bf16)
        return 0

    lax.fori_loop(0, mine.shape[0] // 32, step, 0)


def norm_kernel(half, part, gain, shift_by, *refs):
    normed, centre, scale, normed_t, up_t, turned = refs[-6:]
    tokens, width = part.shape[2:]
    to, rows = pl.ds(half * 4 * tokens, 4 * tokens), width // 8

    def normalise(k, _):
        at = pl.ds(pl.multiple_of(k * tokens, 16), tokens)
        features = part[k, 0].astype(f32)
        mean = jnp.mean(features, axis=1, keepdims=True)
        shifted = features - mean
        inv = lax.rsqrt(jnp.mean(shifted * shifted, axis=1, keepdims=True) + EPSILON)
        normed[at, :] = (shifted * inv * gain[...] + shift_by[...]).astype(bf16)
        centre[at, :] = mean
        scale[at, :] = inv
        return 0

    def turn(c, _):
        lanes = pl.ds(pl.multiple_of(c * 128, 128), 128)
        up_t[lanes, to] = jnp.concatenate([part[k, 1, :, lanes] for k in range(4)], 0).T
        turned[lanes, :] = normed[:, lanes].T
        return 0

    def order(b, _):
        at = pl.multiple_of((lax.rem(b, 2) * 4 + lax.div(b, 2)) * rows, 16)
        normed_t[pl.ds(at, rows), to] = turned[pl.ds(pl.multiple_of(b * rows, 16), rows), :]
        return 0

    lax.fori_loop(0, 4, normalise, 0)
    lax.fori_loop(0, width // 128, turn, 0)
    lax.fori_loop(0, 8, order, 0)


def hidden_kernel(half, part, normed, expand, shrink, bias, *refs):
    bias_sum, active, back, pre_tile, back_tile = refs[-5:]
    tokens, width = part.shape[2:]
    tile, to = 256, pl.ds(half * 4 * tokens, 4 * tokens)
    tiles = expand.shape[1] // tile

    def lanes_of(j):
        return pl.ds(pl.multiple_of(j * tile, tile), tile)

    def products(j, slot):
        lanes = lanes_of(j)
        pre_tile[slot] = dot(normed[...], expand[:, lanes])
        back_tile[slot] = dot(jnp.concatenate([part[k, 1] for k in range(4)], 0), shrink[:, lanes])

    def finish(j, slot):
        lanes = lanes_of(j)
        value, slope = gelu_parts(pre_tile[slot] + bias[:, lanes])
        active[to, lanes] = value.astype(bf16)
        grad = (back_tile[slot] * slope).astype(bf16)
        back[to, lanes] = grad
        bias_sum[:, lanes] = jnp.sum(grad.astype(f32), axis=0, keepdims=True)

    def step(j, _):
        products(2 * j + 1, 1)
        finish(2 * j, 0)
        following = lax.rem(2 * j + 2, tiles)
        products(following, 0)
        finish(2 * j + 1, 1)
        return 0

    products(0, 0)
    lax.fori_loop(0, tiles // 2, step, 0)


def second_kernel(part, gain, shift_by, bias, expand, shrink, normed_t_in, up_t_in, active_in, back_in, *refs):
    centre, scale, normed_t, up_t, bias_sum, active, back, normed, turned, pre_tile, back_tile = refs
    norm_kernel(1, part, gain, shift_by, normed, centre, scale, normed_t, up_t, turned)
    hidden_kernel(1, part, normed, expand, shrink, bias, bias_sum, active, back, pre_tile, back_tile)


def shrink_tile(far, n, up_t, active):
    x, _ = place()
    rows, lanes = up_t.shape[0] // 4, pl.ds(pl.multiple_of(n * 256, 256), 256)
    return lanes, dot(up_t[pl.ds(pl.multiple_of(lax.rem(x + far, 4) * rows, 16), rows), :], active[:, lanes])


def expand_tile(far, n, normed_t, back):
    _, y = place()
    py = lax.rem(y + far, 4)
    rows, half = normed_t.shape[0] // 2, back.shape[1] // 2
    right = back[:, pl.ds(pl.multiple_of(lax.rem(py, 2) * half + n * 256, 256), 256)]
    left = normed_t[pl.ds(pl.multiple_of(lax.div(py, 2) * rows, 16), rows), :]
    return pl.ds(pl.multiple_of(n * 256, 256), 256), dot(left, right)


def far_kernel(up_t, active, normed_t, back, sums, bias, shrink_low, shrink_high, expand_low, expand_high, vector):
    def tile_of(make, left, right, low, high):
        def step(n, _):
            lanes, term = make(2, n, left, right)
            rows = term.shape[0] // 2
            low[pl.ds(0, rows), lanes] = term[:rows].astype(bf16)
            high[pl.ds(0, rows), lanes] = term[rows:].astype(bf16)
            return 0

        return step

    lax.fori_loop(0, active.shape[1] // 256, tile_of(shrink_tile, up_t, active, shrink_low, shrink_high), 0)
    lax.fori_loop(0, back.shape[1] // 512, tile_of(expand_tile, normed_t, back, expand_low, expand_high), 0)
    hidden, width = bias.shape[1], sums.shape[1]
    vector[...] = jnp.zeros_like(vector)
    for i in range(2):
        for j, start in enumerate(range(0, width, hidden)):
            size = min(hidden, width - start)
            vector[2 * i + j : 2 * i + j + 1, :size] = sums[i : i + 1, start : start + size]
    vector[4:5, :] = bias[...]
    high = vector[...].astype(bf16)
    riding = jnp.concatenate([high, (vector[...] - high.astype(f32)).astype(bf16)], 0)
    for to in (shrink_low, shrink_high):
        to[to.shape[0] - 32 :, :] = riding
    vector[...] = riding[:16].astype(f32) + riding[16:].astype(f32)


def near_kernel(up_t, active, normed_t, back, shrink_own, expand_own, shrink_terms, expand_terms):
    def tile_of(make, left, right, own, terms):
        def for_own(n, _):
            lanes, term = make(0, n, left, right)
            own[:, lanes] = term
            return 0

        def for_others(i, _):
            d, n = lax.rem(i, 2), lax.div(i, 2)
            lanes, term = make(1 + 2 * d, n, left, right)
            terms[d, :, lanes] = term
            return 0

        return for_own, for_others

    for make, left, right, own, terms in (
        (shrink_tile, up_t, active, shrink_own, shrink_terms),
        (expand_tile, normed_t, back, expand_own, expand_terms),
    ):
        tiles = own.shape[1] // 256
        for_own, for_others = tile_of(make, left, right, own, terms)
        lax.fori_loop(0, 2 * tiles, for_others, 0)
        lax.fori_loop(0, tiles, for_own, 0)


def pass_kernel(s_terms, e_terms, s_low, s_high, e_low, e_high, s_ahead, s_behind, e_ahead, e_behind):
    for terms, low, high, ahead, behind in (
        (s_terms, s_low, s_high, s_ahead, s_behind),
        (e_terms, e_low, e_high, e_ahead, e_behind),
    ):
        rows = terms.shape[1] // 2

        def step(i, _, rows=rows, terms=terms, low=low, high=high, ahead=ahead, behind=behind):
            at, then = pl.ds(pl.multiple_of(i * 16, 16), 16), pl.ds(pl.multiple_of(rows + i * 16, 16), 16)
            ahead[at, :] = (terms[0, at, :] + low[at, :].astype(f32)).astype(bf16)
            ahead[then, :] = terms[0, then, :].astype(bf16)
            behind[at, :] = terms[1, at, :].astype(bf16)
            behind[then, :] = (terms[1, then, :] + high[at, :].astype(f32)).astype(bf16)
            return 0

        lax.fori_loop(0, rows // 16, step, 0)
    rows = s_terms.shape[1]
    s_ahead[rows:, :] = s_low[rows // 2 :, :]


def finish_shrink_kernel(own, prev, following, low, high, vector, mine, ahead, far, behind, sums, laid):
    _, y = place()
    rows, half = mine.shape
    wide = own.shape[0]

    def block(by):
        py = lax.rem(y + by, 4)
        at = pl.ds(pl.multiple_of(lax.div(py, 2) * rows, 16), rows)
        lanes = pl.ds(pl.multiple_of(lax.rem(py, 2) * half, 128), half)
        return own[at, lanes] + prev[at, lanes].astype(f32) + following[at, lanes].astype(f32)

    v_prev, v_next, v_far = (from_parts(part[part.shape[0] - 32 :, :]) for part in (low, high, prev))
    total = (vector[...] + v_far) + (v_prev + v_next)
    laid[...] = jnp.zeros_like(laid)
    for r in range(5):
        for k in range(2):
            laid[2 * r + k : 2 * r + k + 1, :] = total[r : r + 1, k * half : (k + 1) * half]
    top = laid[...].astype(bf16)
    riding = jnp.concatenate([top, (laid[...] - top.astype(f32)).astype(bf16)], 0)
    sums[...] = from_parts(riding)
    mine[...] = block(0)
    for by, to in ((1, ahead), (2, far), (3, behind)):
        to[:rows, :] = block(by).astype(bf16)
        to[rows:, :] = riding


def finish_expand_kernel(own, prev, following, mine, ahead, far, behind):
    x, _ = place()
    rows = mine.shape[0]

    def block(by):
        at = pl.ds(pl.multiple_of(lax.rem(x + by, 4) * rows, 16), rows)
        return own[at, :] + prev[at, :].astype(f32) + following[at, :].astype(f32)

    mine[...] = block(0)
    for by, to in ((1, ahead), (2, far), (3, behind)):
        to[...] = block(by).astype(bf16)


def middle_kernel(mine, ahead, behind, total):
    total[...] = mine[...] + ahead[...].astype(f32) + behind[...].astype(f32)


def last_kernel(mine, *refs):
    if len(refs) == 3:
        got, (kept, given) = refs[:1], refs[1:]
    else:
        got, own, (kept, given, sums) = refs[:3], refs[3], refs[4:]
        v_ahead, v_far, v_behind = (from_parts(part[part.shape[0] - 32 :, :]) for part in got)
        sums[...] = (own[...] + v_far) + (v_ahead + v_behind)
    rows = mine.shape[0]
    total = mine[...]
    for part in got:
        total = total + part[:rows, :].astype(f32)
    core = lax.axis_index("core")
    top, bottom = total[: rows // 2], total[rows // 2 :]
    kept[...] = jnp.where(core == 0, top, bottom)
    given[...] = jnp.where(core == 0, bottom, top)


def inputs_kernel(inputs, upstream, grad, gain, result):
    tokens, width = inputs.shape

    def step(i, _):
        at = pl.ds(pl.multiple_of(i * 32, 32), 32)
        features = inputs[at, :].astype(f32)
        shifted = features - jnp.mean(features, axis=1, keepdims=True)
        scale = lax.rsqrt(jnp.mean(shifted * shifted, axis=1, keepdims=True) + EPSILON)
        normed = shifted * scale
        weighted = grad[at, :].astype(f32) * gain[...]
        mean_one = jnp.mean(weighted, axis=1, keepdims=True)
        mean_two = jnp.mean(weighted * normed, axis=1, keepdims=True)
        change = scale * (weighted - mean_one - normed * mean_two)
        result[at, :] = (upstream[at, :].astype(f32) + change).astype(bf16)
        return 0

    lax.fori_loop(0, tokens // 32, step, 0)


def rows_kernel(near, other, near_centre, other_centre, near_scale, other_scale, back, expand, mine, others, sums):
    tokens, width = near.shape[2:]

    def tile_of(lanes):
        gain = plain = 0.0
        for half, part, centre, scale in ((1, other, other_centre, other_scale), (0, near, near_centre, near_scale)):
            rows = dot(back[pl.ds(half * 4 * tokens, 4 * tokens), :], expand[lanes, :], ((1,), (1,)))
            features = jnp.concatenate([part[k, 0, :, lanes] for k in range(4)], 0).astype(f32)
            normed = (features - centre[...]) * scale[...]
            gain = gain + jnp.sum(rows * normed, axis=0, keepdims=True)
            plain = plain + jnp.sum(rows, axis=0, keepdims=True)
            if half:
                others[:, lanes] = rows.astype(bf16)
            else:
                mine[:, lanes] = rows
        sums[0:1, lanes] = gain
        sums[1:2, lanes] = plain

    def step(j, _):
        tile_of(pl.ds(pl.multiple_of(j * 256, 256), 256))
        return 0

    whole = width // 256
    lax.fori_loop(0, whole, step, 0)
    if width % 256:
        tile_of(slice(whole * 256, width))


def local(inputs, upstream, norm_gain, norm_shift, expand_weight, expand_bias, shrink_weight):
    tokens, width = inputs.shape
    rows, hidden = expand_weight.shape
    half = hidden // 2
    x, ylo, z, yhi, core = (lax.axis_index(name) for name in AXES)
    y = 2 * yhi + ylo

    def by_core(weight):
        kept = lax.dynamic_slice_in_dim(weight, core * half, half, 1)
        given = swap(lax.dynamic_slice_in_dim(weight, (1 - core) * half, half, 1))
        return jnp.where(core == 0, jnp.concatenate([kept, given], 0), jnp.concatenate([given, kept], 0))

    block_rows = 2 * rows

    bias_near = lax.ppermute(expand_bias, "ylo", [(0, 1), (1, 0)])
    a, b = by_core(expand_weight), by_core(shrink_weight)

    (stacked,) = call(stack_kernel, [((1, 2, tokens, width), bf16)], (inputs, upstream))
    near = lax.all_gather(stacked, "z", axis=0, tiled=True)

    (a_left, a_right), (b_left, b_right) = both_ways(a, a, "x"), both_ways(b, b, "y")
    a_low, a_high = both_ways(a_left[:rows], a_right[rows:], "x")
    b_low, b_high = both_ways(b_left[:rows], b_right[rows:], "y")
    a = jnp.concatenate([a, a_right, a_low, a_high, a_left], 0)
    a, bias_near = lax.optimization_barrier((a, bias_near))
    b = jnp.concatenate([b, b_right, b_low, b_high, b_left], 0)
    (a_left, a_right), (b_left, b_right) = both_ways(a, a, "y"), both_ways(b, b, "x")
    halves = a_left[: 2 * block_rows], a_right[2 * block_rows :], b_left[: 2 * block_rows], b_right[2 * block_rows :]
    a_low, a_high = both_ways(*halves[:2], "y")
    b_low, b_high = both_ways(*halves[2:], "x")
    pieces = (a, a_right, a_low, a_high, a_left), (b, b_right, b_low, b_high, b_left)
    bias_both = jnp.where(ylo == 0, jnp.stack([expand_bias, bias_near]), jnp.stack([bias_near, expand_bias]))
    bias_own = lax.dynamic_slice_in_dim(bias_both, core * half, half, 1).reshape(1, 2 * half)

    (mark,) = call(nothing_kernel, [], (a_low, a_high, b_low, b_high), mark=True)
    near, mark = lax.optimization_barrier((near, mark))
    other = swap(near)
    many = 8 * tokens
    tall, wide = ((width, many), bf16), ((many, 2 * half), bf16)
    column, half_tall, bias_row = ((4 * tokens, 1), f32), (4 * tokens, width), ((1, 2 * half), f32)
    weight = ((width, 2 * half), bf16)
    gain, shift_by = norm_gain[None], norm_shift[None]
    tile = pltpu.VMEM((2, 4 * tokens, 256), f32)
    turned = pltpu.VMEM((width, 4 * tokens), bf16)
    normed, near_centre, near_scale, normed_t, up_t, mark = call(
        functools.partial(norm_kernel, 0),
        [(half_tall, bf16), column, column, tall, tall],
        (near, gain, shift_by),
        scratch=[turned],
        behind=(mark,),
        mark=True,
    )
    expand_all, shrink_all = (
        call(functools.partial(assemble_kernel, first), [weight], part, behind=(mark,))[0]
        for first, part in zip("xy", pieces, strict=True)
    )
    near_bias, active, back = call(
        functools.partial(hidden_kernel, 0),
        [bias_row, wide, wide],
        (near, normed, expand_all, shrink_all, bias_own),
        scratch=[tile, tile],
    )
    other_centre, other_scale, normed_t, up_t, other_bias, active, back = call(
        second_kernel,
        [column, column, tall, tall, bias_row, wide, wide],
        (other, gain, shift_by, bias_own, expand_all, shrink_all, normed_t, up_t, active, back),
        scratch=[pltpu.VMEM(half_tall, bf16), turned, tile, tile],
        aliases={6: 2, 7: 3, 8: 5, 9: 6},
    )
    bias_part = near_bias + other_bias

    mine, others, norm_sums = call(
        rows_kernel,
        [((4 * tokens, width), f32), ((4 * tokens, width), bf16), ((2, width), f32)],
        (near, other, near_centre, other_centre, near_scale, other_scale, back, expand_all),
    )

    short, long = ((block_rows + 32, 2 * half), bf16), ((2 * block_rows, half), bf16)
    s_low, s_high, e_low, e_high, vector = call(
        far_kernel,
        [short, short, long, long, ((16, 2 * half), f32)],
        (up_t, active, normed_t, back, norm_sums, bias_part),
    )
    (s_low, s_high), (e_low, e_high) = both_ways(s_low, s_high, "x"), both_ways(e_low, e_high, "y")

    both, mark = call(add_kernel, [((4 * tokens, width), bf16)], (mine, swap(others)), behind=(vector,), mark=True)

    s_wide, e_wide = (2 * block_rows, 2 * half), (4 * block_rows, half)
    s_own, e_own, s_terms, e_terms = call(
        near_kernel,
        [(s_wide, f32), (e_wide, f32), ((2, *s_wide), f32), ((2, *e_wide), f32)],
        (up_t, active, normed_t, back),
        behind=(mark,),
    )
    s_ahead, s_behind, e_ahead, e_behind, mark = call(
        pass_kernel,
        [((2 * block_rows + 32, 2 * half), bf16), (s_wide, bf16), (e_wide, bf16), (e_wide, bf16)],
        (s_terms, e_terms, s_low, s_high, e_low, e_high),
        mark=True,
    )
    (s_prev, s_next), (e_prev, e_next) = both_ways(s_ahead, s_behind, "x"), both_ways(e_ahead, e_behind, "y")

    both, pass_mark = lax.optimization_barrier((both, mark))
    grad_normed = lax.psum_scatter(both, "z", scatter_dimension=0, tiled=True)

    block, riding = (block_rows, half), ((block_rows + 32, half), bf16)
    s_mine, *s_blocks, vector = call(
        finish_shrink_kernel,
        [(block, f32), riding, riding, riding, ((16, half), f32)],
        (s_own, s_prev, s_next, s_low, s_high, vector),
        scratch=[pltpu.VMEM((16, half), f32)],
        behind=(pass_mark,),
    )
    s_got = direct(*s_blocks, "y")
    e_mine, *e_blocks = call(finish_expand_kernel, [(block, f32)] + [(block, bf16)] * 3, (e_own, e_prev, e_next))
    e_ahead, e_far, e_behind = direct(*e_blocks, "x")
    inputs_grad, done = call(
        inputs_kernel, [((tokens, width), bf16)], (inputs, upstream, grad_normed, norm_gain[None]), mark=True
    )
    e_mine, mark = call(middle_kernel, [(block, f32)], (e_mine, e_ahead, e_far), behind=(done,), mark=True)
    part = ((rows, half), f32)
    s_kept, s_given, vector = call(last_kernel, [part, part, ((16, half), f32)], (s_mine, *s_got, vector), behind=(mark,))
    e_kept, e_given = call(last_kernel, [part, part], (e_mine, e_behind))

    def by_rows(kept, given):
        got = swap(given)
        return jnp.where(core == 0, jnp.concatenate([kept, got], 1), jnp.concatenate([got, kept], 1))

    shrink_grad, expand_grad = by_rows(s_kept, s_given), by_rows(e_kept, e_given)
    norm_sums = pair_sum(vector[:8], "z")
    norm_sums = norm_sums + swap(norm_sums)
    gain_grad, shift_grad = (norm_sums[i : i + 4].reshape(-1)[:width] for i in (0, 4))
    bias_mine = lax.dynamic_index_in_dim(vector, 8 + ylo, 0, keepdims=False)
    bias_other = swap(bias_mine)
    bias_grad = jnp.where(
        core == 0, jnp.concatenate([bias_mine, bias_other]), jnp.concatenate([bias_other, bias_mine])
    )
    return inputs_grad, gain_grad, shift_grad, expand_grad, bias_grad, shrink_grad


def solution(mesh):
    fine = Mesh(mesh.devices.reshape(4, 2, 4, 2, 2), AXES)
    by_token = P(AXES, None)
    by_weight = P(("x", "yhi", "core"), ("ylo", "z"))
    by_hidden = P(("ylo", "z"))
    return jax.shard_map(
        local,
        mesh=fine,
        in_specs=(by_token, by_token, P(), P(), by_weight, by_hidden, by_weight),
        out_specs=(by_token, P(), P(), by_weight, by_hidden, by_weight),
        check_vma=False,
    )
```

```python
import functools

import jax
import jax.numpy as jnp
from jax import lax
from jax.experimental import pallas as pl
from jax.experimental.pallas import tpu as pltpu
from jax.sharding import Mesh, PartitionSpec as P

EPSILON = 1e-06
ROOT_HALF = 0.7071067811865476
INV_ROOT_TWO_PI = 0.3989422804014327

AXES = ("x", "ylo", "z", "yhi", "core")
PLANE_Y = ("ylo", "yhi")
f32, bf16 = jnp.float32, jnp.bfloat16


def y_index(y):
    return (y % 2) * 2 + y // 2


def shift(value, axis, by):
    if axis == "y":
        pairs = [(y_index(y), y_index((y + by) % 4)) for y in range(4)]
        return lax.ppermute(value, PLANE_Y, pairs)
    return lax.ppermute(value, axis, [(i, (i + by) % 4) for i in range(4)])


def swap(value):
    return lax.ppermute(value, "core", [(0, 1), (1, 0)])


def after(value, *others):
    return lax.optimization_barrier((value, *others))[0]


def both_ways(ahead, behind, axis):
    return shift(ahead, axis, 1), shift(behind, axis, -1)


def pair_sum(value, axis):
    for bit in (1, 2):
        value = value + lax.ppermute(value, axis, [(i, i ^ bit) for i in range(4)])
    return value


def from_parts(rows):
    return rows[:16].astype(f32) + rows[16:].astype(f32)


def direct(ahead, far, behind, axis):
    return shift(ahead, axis, 1), shift(far, axis, 2), shift(behind, axis, 3)


def assemble_kernel(first, own, right, far_low, far_high, left, whole):
    x, y = place()
    rows, half = own.shape[0] // 4, own.shape[1]
    for far_second in range(4):
        for far_first in range(4):
            if far_second == 2:
                bundle, at = (far_low, far_first) if far_first < 2 else (far_high, far_first - 2)
            else:
                bundle, at = {0: own, 1: right, 3: left}[far_second], far_first
            far_x, far_y = (far_first, far_second) if first == "x" else (far_second, far_first)
            px, py = lax.rem(x + far_x, 4), lax.rem(y + far_y, 4)
            row = pl.multiple_of((2 * px + lax.div(py, 2)) * rows, 16)
            column = pl.multiple_of(lax.rem(py, 2) * half, 128)
            whole[pl.ds(row, rows), pl.ds(column, half)] = bundle[at * rows : (at + 1) * rows, :]


def place():
    return lax.axis_index("x"), 2 * lax.axis_index("yhi") + lax.axis_index("ylo")


def gelu_parts(pre):
    cdf = 0.5 * (1.0 + lax.erf(pre * ROOT_HALF))
    density = INV_ROOT_TWO_PI * jnp.exp(-0.5 * pre * pre)
    return pre * cdf, cdf + pre * density


def dot(left, right, dims=((1,), (0,))):
    return lax.dot_general(left, right, (dims, ((), ())), preferred_element_type=f32)


def call(kernel, outs, args, scratch=(), aliases=None, behind=(), mark=False, limit=16):
    given, made = len(args), len(outs)

    def body(*refs):
        refs = refs[:given] + refs[given + len(behind) :]
        if mark:
            refs[given + made][...] = jnp.zeros_like(refs[given + made])
            refs = refs[: given + made] + refs[given + made + 1 :]
        kernel(*refs)

    outs = [*outs, *[((8, 128), f32)] * mark]
    whole = pl.BlockSpec(memory_space=pltpu.VMEM)
    return pl.pallas_call(
        body,
        out_shape=[jax.ShapeDtypeStruct(shape, dtype) for shape, dtype in outs],
        in_specs=[whole] * (given + len(behind)),
        out_specs=[whole] * len(outs),
        scratch_shapes=list(scratch),
        input_output_aliases=aliases or {},
        compiler_params=pltpu.CompilerParams(vmem_limit_bytes=limit * 2**20),
        cost_estimate=pl.CostEstimate(flops=10**6, bytes_accessed=10**6, transcendentals=0),
    )(*args, *behind)


def stack_kernel(inputs, upstream, stacked):
    stacked[0, 0] = inputs[...]
    stacked[0, 1] = upstream[...]


def add_kernel(mine, others, total):
    def step(i, _):
        at = pl.ds(pl.multiple_of(i * 32, 32), 32)
        total[at, :] = (mine[at, :] + others[at, :].astype(f32)).astype(bf16)
        return 0

    lax.fori_loop(0, mine.shape[0] // 32, step, 0)


def norm_kernel(half, part, gain, shift_by, *refs):
    normed, centre, scale, normed_t, up_t, turned = refs[-6:]
    tokens, width = part.shape[2:]
    to, rows = pl.ds(half * 4 * tokens, 4 * tokens), width // 8

    def normalise(k, _):
        at = pl.ds(pl.multiple_of(k * tokens, 16), tokens)
        features = part[k, 0].astype(f32)
        mean = jnp.mean(features, axis=1, keepdims=True)
        shifted = features - mean
        inv = lax.rsqrt(jnp.mean(shifted * shifted, axis=1, keepdims=True) + EPSILON)
        normed[at, :] = (shifted * inv * gain[...] + shift_by[...]).astype(bf16)
        centre[at, :] = mean
        scale[at, :] = inv
        return 0

    def turn(c, _):
        lanes = pl.ds(pl.multiple_of(c * 128, 128), 128)
        up_t[lanes, to] = jnp.concatenate([part[k, 1, :, lanes] for k in range(4)], 0).T
        turned[lanes, :] = normed[:, lanes].T
        return 0

    def order(b, _):
        at = pl.multiple_of((lax.rem(b, 2) * 4 + lax.div(b, 2)) * rows, 16)
        normed_t[pl.ds(at, rows), to] = turned[pl.ds(pl.multiple_of(b * rows, 16), rows), :]
        return 0

    lax.fori_loop(0, 4, normalise, 0)
    lax.fori_loop(0, width // 128, turn, 0)
    lax.fori_loop(0, 8, order, 0)


def hidden_kernel(half, part, normed, expand, shrink, bias, *refs):
    bias_sum, active, back, pre_tile, back_tile = refs[-5:]
    tokens, width = part.shape[2:]
    tile, to = 256, pl.ds(half * 4 * tokens, 4 * tokens)
    tiles = expand.shape[1] // tile

    def lanes_of(j):
        return pl.ds(pl.multiple_of(j * tile, tile), tile)

    def products(j, slot):
        lanes = lanes_of(j)
        pre_tile[slot] = dot(normed[...], expand[:, lanes])
        back_tile[slot] = dot(jnp.concatenate([part[k, 1] for k in range(4)], 0), shrink[:, lanes])

    def finish(j, slot):
        lanes = lanes_of(j)
        value, slope = gelu_parts(pre_tile[slot] + bias[:, lanes])
        active[to, lanes] = value.astype(bf16)
        grad = (back_tile[slot] * slope).astype(bf16)
        back[to, lanes] = grad
        bias_sum[:, lanes] = jnp.sum(grad.astype(f32), axis=0, keepdims=True)

    def step(j, _):
        products(2 * j + 1, 1)
        finish(2 * j, 0)
        following = lax.rem(2 * j + 2, tiles)
        products(following, 0)
        finish(2 * j + 1, 1)
        return 0

    products(0, 0)
    lax.fori_loop(0, tiles // 2, step, 0)


def second_kernel(part, gain, shift_by, bias, expand, shrink, normed_t_in, up_t_in, active_in, back_in, *refs):
    centre, scale, normed_t, up_t, bias_sum, active, back, normed, turned, pre_tile, back_tile = refs
    norm_kernel(1, part, gain, shift_by, normed, centre, scale, normed_t, up_t, turned)
    hidden_kernel(1, part, normed, expand, shrink, bias, bias_sum, active, back, pre_tile, back_tile)


def shrink_tile(far, n, up_t, active):
    x, _ = place()
    rows, lanes = up_t.shape[0] // 4, pl.ds(pl.multiple_of(n * 256, 256), 256)
    return lanes, dot(up_t[pl.ds(pl.multiple_of(lax.rem(x + far, 4) * rows, 16), rows), :], active[:, lanes])


def expand_tile(far, n, normed_t, back):
    _, y = place()
    py = lax.rem(y + far, 4)
    rows, half = normed_t.shape[0] // 2, back.shape[1] // 2
    right = back[:, pl.ds(pl.multiple_of(lax.rem(py, 2) * half + n * 256, 256), 256)]
    left = normed_t[pl.ds(pl.multiple_of(lax.div(py, 2) * rows, 16), rows), :]
    return pl.ds(pl.multiple_of(n * 256, 256), 256), dot(left, right)


def far_kernel(up_t, active, normed_t, back, sums, bias, shrink_low, shrink_high, expand_low, expand_high, vector):
    def tile_of(make, left, right, low, high):
        def step(n, _):
            lanes, term = make(2, n, left, right)
            rows = term.shape[0] // 2
            low[pl.ds(0, rows), lanes] = term[:rows].astype(bf16)
            high[pl.ds(0, rows), lanes] = term[rows:].astype(bf16)
            return 0

        return step

    lax.fori_loop(0, active.shape[1] // 256, tile_of(shrink_tile, up_t, active, shrink_low, shrink_high), 0)
    lax.fori_loop(0, back.shape[1] // 512, tile_of(expand_tile, normed_t, back, expand_low, expand_high), 0)
    hidden, width = bias.shape[1], sums.shape[1]
    vector[...] = jnp.zeros_like(vector)
    for i in range(2):
        for j, start in enumerate(range(0, width, hidden)):
            size = min(hidden, width - start)
            vector[2 * i + j : 2 * i + j + 1, :size] = sums[i : i + 1, start : start + size]
    vector[4:5, :] = bias[...]
    high = vector[...].astype(bf16)
    riding = jnp.concatenate([high, (vector[...] - high.astype(f32)).astype(bf16)], 0)
    for to in (shrink_low, shrink_high):
        to[to.shape[0] - 32 :, :] = riding
    vector[...] = riding[:16].astype(f32) + riding[16:].astype(f32)


def near_kernel(up_t, active, normed_t, back, shrink_own, expand_own, shrink_terms, expand_terms):
    def tile_of(make, left, right, own, terms):
        def for_own(n, _):
            lanes, term = make(0, n, left, right)
            own[:, lanes] = term
            return 0

        def for_others(i, _):
            d, n = lax.rem(i, 2), lax.div(i, 2)
            lanes, term = make(1 + 2 * d, n, left, right)
            terms[d, :, lanes] = term
            return 0

        return for_own, for_others

    for make, left, right, own, terms in (
        (shrink_tile, up_t, active, shrink_own, shrink_terms),
        (expand_tile, normed_t, back, expand_own, expand_terms),
    ):
        tiles = own.shape[1] // 256
        for_own, for_others = tile_of(make, left, right, own, terms)
        lax.fori_loop(0, 2 * tiles, for_others, 0)
        lax.fori_loop(0, tiles, for_own, 0)


def pass_kernel(s_terms, e_terms, s_low, s_high, e_low, e_high, s_ahead, s_behind, e_ahead, e_behind):
    for terms, low, high, ahead, behind in (
        (s_terms, s_low, s_high, s_ahead, s_behind),
        (e_terms, e_low, e_high, e_ahead, e_behind),
    ):
        rows = terms.shape[1] // 2

        def step(i, _, rows=rows, terms=terms, low=low, high=high, ahead=ahead, behind=behind):
            at, then = pl.ds(pl.multiple_of(i * 16, 16), 16), pl.ds(pl.multiple_of(rows + i * 16, 16), 16)
            ahead[at, :] = (terms[0, at, :] + low[at, :].astype(f32)).astype(bf16)
            ahead[then, :] = terms[0, then, :].astype(bf16)
            behind[at, :] = terms[1, at, :].astype(bf16)
            behind[then, :] = (terms[1, then, :] + high[at, :].astype(f32)).astype(bf16)
            return 0

        lax.fori_loop(0, rows // 16, step, 0)
    rows = s_terms.shape[1]
    s_ahead[rows:, :] = s_low[rows // 2 :, :]


def finish_shrink_kernel(own, prev, following, low, high, vector, mine, ahead, far, behind, sums, laid):
    _, y = place()
    rows, half = mine.shape
    wide = own.shape[0]

    def block(by):
        py = lax.rem(y + by, 4)
        at = pl.ds(pl.multiple_of(lax.div(py, 2) * rows, 16), rows)
        lanes = pl.ds(pl.multiple_of(lax.rem(py, 2) * half, 128), half)
        return own[at, lanes] + prev[at, lanes].astype(f32) + following[at, lanes].astype(f32)

    v_prev, v_next, v_far = (from_parts(part[part.shape[0] - 32 :, :]) for part in (low, high, prev))
    total = (vector[...] + v_far) + (v_prev + v_next)
    laid[...] = jnp.zeros_like(laid)
    for r in range(5):
        for k in range(2):
            laid[2 * r + k : 2 * r + k + 1, :] = total[r : r + 1, k * half : (k + 1) * half]
    top = laid[...].astype(bf16)
    riding = jnp.concatenate([top, (laid[...] - top.astype(f32)).astype(bf16)], 0)
    sums[...] = from_parts(riding)
    mine[...] = block(0)
    for by, to in ((1, ahead), (2, far), (3, behind)):
        to[:rows, :] = block(by).astype(bf16)
        to[rows:, :] = riding


def finish_expand_kernel(own, prev, following, mine, ahead, far, behind):
    x, _ = place()
    rows = mine.shape[0]

    def block(by):
        at = pl.ds(pl.multiple_of(lax.rem(x + by, 4) * rows, 16), rows)
        return own[at, :] + prev[at, :].astype(f32) + following[at, :].astype(f32)

    mine[...] = block(0)
    for by, to in ((1, ahead), (2, far), (3, behind)):
        to[...] = block(by).astype(bf16)


def middle_kernel(mine, ahead, behind, total):
    total[...] = mine[...] + ahead[...].astype(f32) + behind[...].astype(f32)


def last_kernel(mine, *refs):
    if len(refs) == 3:
        got, (kept, given) = refs[:1], refs[1:]
    else:
        got, own, (kept, given, sums) = refs[:3], refs[3], refs[4:]
        v_ahead, v_far, v_behind = (from_parts(part[part.shape[0] - 32 :, :]) for part in got)
        sums[...] = (own[...] + v_far) + (v_ahead + v_behind)
    rows = mine.shape[0]
    total = mine[...]
    for part in got:
        total = total + part[:rows, :].astype(f32)
    core = lax.axis_index("core")
    top, bottom = total[: rows // 2], total[rows // 2 :]
    kept[...] = jnp.where(core == 0, top, bottom)
    given[...] = jnp.where(core == 0, bottom, top)


def inputs_kernel(inputs, upstream, grad, gain, result):
    tokens, width = inputs.shape

    def step(i, _):
        at = pl.ds(pl.multiple_of(i * 32, 32), 32)
        features = inputs[at, :].astype(f32)
        shifted = features - jnp.mean(features, axis=1, keepdims=True)
        scale = lax.rsqrt(jnp.mean(shifted * shifted, axis=1, keepdims=True) + EPSILON)
        normed = shifted * scale
        weighted = grad[at, :].astype(f32) * gain[...]
        mean_one = jnp.mean(weighted, axis=1, keepdims=True)
        mean_two = jnp.mean(weighted * normed, axis=1, keepdims=True)
        change = scale * (weighted - mean_one - normed * mean_two)
        result[at, :] = (upstream[at, :].astype(f32) + change).astype(bf16)
        return 0

    lax.fori_loop(0, tokens // 32, step, 0)


def rows_kernel(near, other, near_centre, other_centre, near_scale, other_scale, back, expand, mine, others, sums):
    tokens, width = near.shape[2:]

    def tile_of(lanes):
        gain = plain = 0.0
        for half, part, centre, scale in ((1, other, other_centre, other_scale), (0, near, near_centre, near_scale)):
            rows = dot(back[pl.ds(half * 4 * tokens, 4 * tokens), :], expand[lanes, :], ((1,), (1,)))
            features = jnp.concatenate([part[k, 0, :, lanes] for k in range(4)], 0).astype(f32)
            normed = (features - centre[...]) * scale[...]
            gain = gain + jnp.sum(rows * normed, axis=0, keepdims=True)
            plain = plain + jnp.sum(rows, axis=0, keepdims=True)
            if half:
                others[:, lanes] = rows.astype(bf16)
            else:
                mine[:, lanes] = rows
        sums[0:1, lanes] = gain
        sums[1:2, lanes] = plain

    def step(j, _):
        tile_of(pl.ds(pl.multiple_of(j * 256, 256), 256))
        return 0

    whole = width // 256
    lax.fori_loop(0, whole, step, 0)
    if width % 256:
        tile_of(slice(whole * 256, width))


def local(inputs, upstream, norm_gain, norm_shift, expand_weight, expand_bias, shrink_weight):
    tokens, width = inputs.shape
    rows, hidden = expand_weight.shape
    half = hidden // 2
    x, ylo, z, yhi, core = (lax.axis_index(name) for name in AXES)
    y = 2 * yhi + ylo

    def by_core(weight):
        kept = lax.dynamic_slice_in_dim(weight, core * half, half, 1)
        given = swap(lax.dynamic_slice_in_dim(weight, (1 - core) * half, half, 1))
        return jnp.where(core == 0, jnp.concatenate([kept, given], 0), jnp.concatenate([given, kept], 0))

    block_rows = 2 * rows

    bias_near = lax.ppermute(expand_bias, "ylo", [(0, 1), (1, 0)])
    a, b = by_core(expand_weight), by_core(shrink_weight)

    (stacked,) = call(stack_kernel, [((1, 2, tokens, width), bf16)], (inputs, upstream))
    near = lax.all_gather(stacked, "z", axis=0, tiled=True)

    (a_left, a_right), (b_left, b_right) = both_ways(a, a, "x"), both_ways(b, b, "y")
    a_low, a_high = both_ways(a_left[:rows], a_right[rows:], "x")
    b_low, b_high = both_ways(b_left[:rows], b_right[rows:], "y")
    a = jnp.concatenate([a, a_right, a_low, a_high, a_left], 0)
    a, bias_near = lax.optimization_barrier((a, bias_near))
    b = jnp.concatenate([b, b_right, b_low, b_high, b_left], 0)
    (a_left, a_right), (b_left, b_right) = both_ways(a, a, "y"), both_ways(b, b, "x")
    halves = a_left[: 2 * block_rows], a_right[2 * block_rows :], b_left[: 2 * block_rows], b_right[2 * block_rows :]
    a_low, a_high = both_ways(*halves[:2], "y")
    b_low, b_high = both_ways(*halves[2:], "x")
    pieces = (a, a_right, a_low, a_high, a_left), (b, b_right, b_low, b_high, b_left)
    bias_both = jnp.where(ylo == 0, jnp.stack([expand_bias, bias_near]), jnp.stack([bias_near, expand_bias]))
    bias_own = lax.dynamic_slice_in_dim(bias_both, core * half, half, 1).reshape(1, 2 * half)

    (expand_all, first_mark), (shrink_all, second_mark) = (
        call(functools.partial(assemble_kernel, first), [((width, 2 * half), bf16)], part, mark=True)
        for first, part in zip("xy", pieces, strict=True)
    )
    near, first_mark, second_mark = lax.optimization_barrier((near, first_mark, second_mark))
    other = swap(near)
    many = 8 * tokens
    tall, wide = ((width, many), bf16), ((many, 2 * half), bf16)
    column, half_tall, bias_row = ((4 * tokens, 1), f32), (4 * tokens, width), ((1, 2 * half), f32)
    gain, shift_by = norm_gain[None], norm_shift[None]
    tile = pltpu.VMEM((2, 4 * tokens, 256), f32)
    turned = pltpu.VMEM((width, 4 * tokens), bf16)
    normed, near_centre, near_scale, normed_t, up_t = call(
        functools.partial(norm_kernel, 0),
        [(half_tall, bf16), column, column, tall, tall],
        (near, gain, shift_by),
        scratch=[turned],
        behind=(first_mark, second_mark),
    )
    near_bias, active, back = call(
        functools.partial(hidden_kernel, 0),
        [bias_row, wide, wide],
        (near, normed, expand_all, shrink_all, bias_own),
        scratch=[tile, tile],
    )
    other_centre, other_scale, normed_t, up_t, other_bias, active, back = call(
        second_kernel,
        [column, column, tall, tall, bias_row, wide, wide],
        (other, gain, shift_by, bias_own, expand_all, shrink_all, normed_t, up_t, active, back),
        scratch=[pltpu.VMEM(half_tall, bf16), turned, tile, tile],
        aliases={6: 2, 7: 3, 8: 5, 9: 6},
    )
    bias_part = near_bias + other_bias

    mine, others, norm_sums = call(
        rows_kernel,
        [((4 * tokens, width), f32), ((4 * tokens, width), bf16), ((2, width), f32)],
        (near, other, near_centre, other_centre, near_scale, other_scale, back, expand_all),
    )

    short, long = ((block_rows + 32, 2 * half), bf16), ((2 * block_rows, half), bf16)
    s_low, s_high, e_low, e_high, vector = call(
        far_kernel,
        [short, short, long, long, ((16, 2 * half), f32)],
        (up_t, active, normed_t, back, norm_sums, bias_part),
    )
    (s_low, s_high), (e_low, e_high) = both_ways(s_low, s_high, "x"), both_ways(e_low, e_high, "y")

    both, mark = call(add_kernel, [((4 * tokens, width), bf16)], (mine, swap(others)), behind=(vector,), mark=True)

    s_wide, e_wide = (2 * block_rows, 2 * half), (4 * block_rows, half)
    s_own, e_own, s_terms, e_terms = call(
        near_kernel,
        [(s_wide, f32), (e_wide, f32), ((2, *s_wide), f32), ((2, *e_wide), f32)],
        (up_t, active, normed_t, back),
        behind=(mark,),
    )
    s_ahead, s_behind, e_ahead, e_behind, mark = call(
        pass_kernel,
        [((2 * block_rows + 32, 2 * half), bf16), (s_wide, bf16), (e_wide, bf16), (e_wide, bf16)],
        (s_terms, e_terms, s_low, s_high, e_low, e_high),
        mark=True,
    )
    (s_prev, s_next), (e_prev, e_next) = both_ways(s_ahead, s_behind, "x"), both_ways(e_ahead, e_behind, "y")

    both, pass_mark = lax.optimization_barrier((both, mark))
    grad_normed = lax.psum_scatter(both, "z", scatter_dimension=0, tiled=True)

    block, riding = (block_rows, half), ((block_rows + 32, half), bf16)
    s_mine, *s_blocks, vector = call(
        finish_shrink_kernel,
        [(block, f32), riding, riding, riding, ((16, half), f32)],
        (s_own, s_prev, s_next, s_low, s_high, vector),
        scratch=[pltpu.VMEM((16, half), f32)],
        behind=(pass_mark,),
    )
    s_got = direct(*s_blocks, "y")
    e_mine, *e_blocks = call(finish_expand_kernel, [(block, f32)] + [(block, bf16)] * 3, (e_own, e_prev, e_next))
    e_ahead, e_far, e_behind = direct(*e_blocks, "x")
    inputs_grad, done = call(
        inputs_kernel, [((tokens, width), bf16)], (inputs, upstream, grad_normed, norm_gain[None]), mark=True
    )
    e_mine, mark = call(middle_kernel, [(block, f32)], (e_mine, e_ahead, e_far), behind=(done,), mark=True)
    part = ((rows, half), f32)
    s_kept, s_given, vector = call(last_kernel, [part, part, ((16, half), f32)], (s_mine, *s_got, vector), behind=(mark,))
    e_kept, e_given = call(last_kernel, [part, part], (e_mine, e_behind))

    def by_rows(kept, given):
        got = swap(given)
        return jnp.where(core == 0, jnp.concatenate([kept, got], 1), jnp.concatenate([got, kept], 1))

    shrink_grad, expand_grad = by_rows(s_kept, s_given), by_rows(e_kept, e_given)
    norm_sums = pair_sum(vector[:8], "z")
    norm_sums = norm_sums + swap(norm_sums)
    gain_grad, shift_grad = (norm_sums[i : i + 4].reshape(-1)[:width] for i in (0, 4))
    bias_mine = lax.dynamic_index_in_dim(vector, 8 + ylo, 0, keepdims=False)
    bias_other = swap(bias_mine)
    bias_grad = jnp.where(
        core == 0, jnp.concatenate([bias_mine, bias_other]), jnp.concatenate([bias_other, bias_mine])
    )
    return inputs_grad, gain_grad, shift_grad, expand_grad, bias_grad, shrink_grad


def solution(mesh):
    fine = Mesh(mesh.devices.reshape(4, 2, 4, 2, 2), AXES)
    by_token = P(AXES, None)
    by_weight = P(("x", "yhi", "core"), ("ylo", "z"))
    by_hidden = P(("ylo", "z"))
    return jax.shard_map(
        local,
        mesh=fine,
        in_specs=(by_token, by_token, P(), P(), by_weight, by_hidden, by_weight),
        out_specs=(by_token, P(), P(), by_weight, by_hidden, by_weight),
        check_vma=False,
    )
```

```python
import functools

import jax
import jax.numpy as jnp
from jax import lax
from jax.experimental import pallas as pl
from jax.experimental.pallas import tpu as pltpu
from jax.sharding import Mesh, PartitionSpec as P

EPSILON = 1e-06
ROOT_HALF = 0.7071067811865476
INV_ROOT_TWO_PI = 0.3989422804014327

AXES = ("x", "ylo", "z", "yhi", "core")
PLANE_Y = ("ylo", "yhi")
f32, bf16 = jnp.float32, jnp.bfloat16


def y_index(y):
    return (y % 2) * 2 + y // 2


def shift(value, axis, by):
    if axis == "y":
        pairs = [(y_index(y), y_index((y + by) % 4)) for y in range(4)]
        return lax.ppermute(value, PLANE_Y, pairs)
    return lax.ppermute(value, axis, [(i, (i + by) % 4) for i in range(4)])


def swap(value):
    return lax.ppermute(value, "core", [(0, 1), (1, 0)])


def after(value, *others):
    return lax.optimization_barrier((value, *others))[0]


def both_ways(ahead, behind, axis):
    return shift(ahead, axis, 1), shift(behind, axis, -1)


def pair_sum(value, axis):
    for bit in (1, 2):
        value = value + lax.ppermute(value, axis, [(i, i ^ bit) for i in range(4)])
    return value


def from_parts(rows):
    return rows[:16].astype(f32) + rows[16:].astype(f32)


def direct(ahead, far, behind, axis):
    return shift(ahead, axis, 1), shift(far, axis, 2), shift(behind, axis, 3)


def assemble_kernel(first, own, right, far_low, far_high, left, whole):
    x, y = place()
    rows, half = own.shape[0] // 4, own.shape[1]
    for far_second in range(4):
        for far_first in range(4):
            if far_second == 2:
                bundle, at = (far_low, far_first) if far_first < 2 else (far_high, far_first - 2)
            else:
                bundle, at = {0: own, 1: right, 3: left}[far_second], far_first
            far_x, far_y = (far_first, far_second) if first == "x" else (far_second, far_first)
            px, py = lax.rem(x + far_x, 4), lax.rem(y + far_y, 4)
            row = pl.multiple_of((2 * px + lax.div(py, 2)) * rows, 16)
            column = pl.multiple_of(lax.rem(py, 2) * half, 128)
            whole[pl.ds(row, rows), pl.ds(column, half)] = bundle[at * rows : (at + 1) * rows, :]


def place():
    return lax.axis_index("x"), 2 * lax.axis_index("yhi") + lax.axis_index("ylo")


def gelu_parts(pre):
    cdf = 0.5 * (1.0 + lax.erf(pre * ROOT_HALF))
    density = INV_ROOT_TWO_PI * jnp.exp(-0.5 * pre * pre)
    return pre * cdf, cdf + pre * density


def dot(left, right, dims=((1,), (0,))):
    return lax.dot_general(left, right, (dims, ((), ())), preferred_element_type=f32)


def call(kernel, outs, args, scratch=(), aliases=None, behind=(), mark=False, limit=16):
    given, made = len(args), len(outs)

    def body(*refs):
        refs = refs[:given] + refs[given + len(behind) :]
        if mark:
            refs[given + made][...] = jnp.zeros_like(refs[given + made])
            refs = refs[: given + made] + refs[given + made + 1 :]
        kernel(*refs)

    outs = [*outs, *[((8, 128), f32)] * mark]
    whole = pl.BlockSpec(memory_space=pltpu.VMEM)
    return pl.pallas_call(
        body,
        out_shape=[jax.ShapeDtypeStruct(shape, dtype) for shape, dtype in outs],
        in_specs=[whole] * (given + len(behind)),
        out_specs=[whole] * len(outs),
        scratch_shapes=list(scratch),
        input_output_aliases=aliases or {},
        compiler_params=pltpu.CompilerParams(vmem_limit_bytes=limit * 2**20),
        cost_estimate=pl.CostEstimate(flops=10**6, bytes_accessed=10**6, transcendentals=0),
    )(*args, *behind)


def stack_kernel(inputs, upstream, stacked):
    stacked[0, 0] = inputs[...]
    stacked[0, 1] = upstream[...]


def add_kernel(mine, others, total):
    def step(i, _):
        at = pl.ds(pl.multiple_of(i * 32, 32), 32)
        total[at, :] = (mine[at, :] + others[at, :].astype(f32)).astype(bf16)
        return 0

    lax.fori_loop(0, mine.shape[0] // 32, step, 0)


def norm_kernel(half, part, gain, shift_by, *refs, unroll=False):
    normed, centre, scale, normed_t, up_t, turned = refs[-6:]
    tokens, width = part.shape[2:]
    to, rows = pl.ds(half * 4 * tokens, 4 * tokens), width // 8

    def normalise(k, _):
        at = pl.ds(pl.multiple_of(k * tokens, 16), tokens)
        features = part[k, 0].astype(f32)
        mean = jnp.mean(features, axis=1, keepdims=True)
        shifted = features - mean
        inv = lax.rsqrt(jnp.mean(shifted * shifted, axis=1, keepdims=True) + EPSILON)
        normed[at, :] = (shifted * inv * gain[...] + shift_by[...]).astype(bf16)
        centre[at, :] = mean
        scale[at, :] = inv
        return 0

    def turn(c, _):
        lanes = pl.ds(pl.multiple_of(c * 128, 128), 128)
        up_t[lanes, to] = jnp.concatenate([part[k, 1, :, lanes] for k in range(4)], 0).T
        turned[lanes, :] = normed[:, lanes].T
        return 0

    def order(b, _):
        at = pl.multiple_of((lax.rem(b, 2) * 4 + lax.div(b, 2)) * rows, 16)
        normed_t[pl.ds(at, rows), to] = turned[pl.ds(pl.multiple_of(b * rows, 16), rows), :]
        return 0

    lax.fori_loop(0, 4, normalise, 0, unroll=unroll)
    lax.fori_loop(0, width // 128, turn, 0, unroll=unroll)
    lax.fori_loop(0, 8, order, 0, unroll=unroll)


def hidden_kernel(half, part, normed, expand, shrink, bias, *refs, unroll=False):
    bias_sum, active, back, pre_tile, back_tile = refs[-5:]
    tokens, width = part.shape[2:]
    tile, to = 256, pl.ds(half * 4 * tokens, 4 * tokens)
    tiles = expand.shape[1] // tile

    def lanes_of(j):
        return slice(j * tile, (j + 1) * tile) if unroll else pl.ds(pl.multiple_of(j * tile, tile), tile)

    def products(j, slot):
        lanes = lanes_of(j)
        pre_tile[slot] = dot(normed[...], expand[:, lanes])
        back_tile[slot] = dot(jnp.concatenate([part[k, 1] for k in range(4)], 0), shrink[:, lanes])

    def finish(j, slot):
        lanes = lanes_of(j)
        value, slope = gelu_parts(pre_tile[slot] + bias[:, lanes])
        active[to, lanes] = value.astype(bf16)
        grad = (back_tile[slot] * slope).astype(bf16)
        back[to, lanes] = grad
        bias_sum[:, lanes] = jnp.sum(grad.astype(f32), axis=0, keepdims=True)

    def step(j, _):
        products(j, 0)
        finish(j, 0)
        return 0

    if unroll:
        products(0, 0)
        for j in range(1, tiles):
            products(j, j % 2)
            finish(j - 1, (j - 1) % 2)
        finish(tiles - 1, (tiles - 1) % 2)
    else:
        lax.fori_loop(0, tiles, step, 0)


def second_kernel(part, gain, shift_by, bias, expand, shrink, normed_t_in, up_t_in, active_in, back_in, *refs):
    centre, scale, normed_t, up_t, bias_sum, active, back, normed, turned, pre_tile, back_tile = refs
    norm_kernel(1, part, gain, shift_by, normed, centre, scale, normed_t, up_t, turned)
    hidden_kernel(1, part, normed, expand, shrink, bias, bias_sum, active, back, pre_tile, back_tile)


def shrink_tile(far, n, up_t, active):
    x, _ = place()
    rows, lanes = up_t.shape[0] // 4, pl.ds(pl.multiple_of(n * 256, 256), 256)
    return lanes, dot(up_t[pl.ds(pl.multiple_of(lax.rem(x + far, 4) * rows, 16), rows), :], active[:, lanes])


def expand_tile(far, n, normed_t, back):
    _, y = place()
    py = lax.rem(y + far, 4)
    rows, half = normed_t.shape[0] // 2, back.shape[1] // 2
    right = back[:, pl.ds(pl.multiple_of(lax.rem(py, 2) * half + n * 256, 256), 256)]
    left = normed_t[pl.ds(pl.multiple_of(lax.div(py, 2) * rows, 16), rows), :]
    return pl.ds(pl.multiple_of(n * 256, 256), 256), dot(left, right)


def far_kernel(up_t, active, normed_t, back, sums, bias, shrink_low, shrink_high, expand_low, expand_high, vector):
    def tile_of(make, left, right, low, high):
        def step(n, _):
            lanes, term = make(2, n, left, right)
            rows = term.shape[0] // 2
            low[pl.ds(0, rows), lanes] = term[:rows].astype(bf16)
            high[pl.ds(0, rows), lanes] = term[rows:].astype(bf16)
            return 0

        return step

    lax.fori_loop(0, active.shape[1] // 256, tile_of(shrink_tile, up_t, active, shrink_low, shrink_high), 0)
    lax.fori_loop(0, back.shape[1] // 512, tile_of(expand_tile, normed_t, back, expand_low, expand_high), 0)
    hidden, width = bias.shape[1], sums.shape[1]
    vector[...] = jnp.zeros_like(vector)
    for i in range(2):
        for j, start in enumerate(range(0, width, hidden)):
            size = min(hidden, width - start)
            vector[2 * i + j : 2 * i + j + 1, :size] = sums[i : i + 1, start : start + size]
    vector[4:5, :] = bias[...]
    high = vector[...].astype(bf16)
    riding = jnp.concatenate([high, (vector[...] - high.astype(f32)).astype(bf16)], 0)
    for to in (shrink_low, shrink_high):
        to[to.shape[0] - 32 :, :] = riding
    vector[...] = riding[:16].astype(f32) + riding[16:].astype(f32)


def near_kernel(up_t, active, normed_t, back, shrink_own, expand_own, shrink_terms, expand_terms):
    def tile_of(make, left, right, own, terms):
        def for_own(n, _):
            lanes, term = make(0, n, left, right)
            own[:, lanes] = term
            return 0

        def for_others(i, _):
            d, n = lax.rem(i, 2), lax.div(i, 2)
            lanes, term = make(1 + 2 * d, n, left, right)
            terms[d, :, lanes] = term
            return 0

        return for_own, for_others

    for make, left, right, own, terms in (
        (shrink_tile, up_t, active, shrink_own, shrink_terms),
        (expand_tile, normed_t, back, expand_own, expand_terms),
    ):
        tiles = own.shape[1] // 256
        for_own, for_others = tile_of(make, left, right, own, terms)
        lax.fori_loop(0, 2 * tiles, for_others, 0)
        lax.fori_loop(0, tiles, for_own, 0)


def pass_kernel(s_terms, e_terms, s_low, s_high, e_low, e_high, s_ahead, s_behind, e_ahead, e_behind):
    for terms, low, high, ahead, behind in (
        (s_terms, s_low, s_high, s_ahead, s_behind),
        (e_terms, e_low, e_high, e_ahead, e_behind),
    ):
        rows = terms.shape[1] // 2

        def step(i, _, rows=rows, terms=terms, low=low, high=high, ahead=ahead, behind=behind):
            at, then = pl.ds(pl.multiple_of(i * 16, 16), 16), pl.ds(pl.multiple_of(rows + i * 16, 16), 16)
            ahead[at, :] = (terms[0, at, :] + low[at, :].astype(f32)).astype(bf16)
            ahead[then, :] = terms[0, then, :].astype(bf16)
            behind[at, :] = terms[1, at, :].astype(bf16)
            behind[then, :] = (terms[1, then, :] + high[at, :].astype(f32)).astype(bf16)
            return 0

        lax.fori_loop(0, rows // 16, step, 0)
    rows = s_terms.shape[1]
    s_ahead[rows:, :] = s_low[rows // 2 :, :]


def finish_shrink_kernel(own, prev, following, low, high, vector, mine, ahead, far, behind, sums, laid):
    _, y = place()
    rows, half = mine.shape
    wide = own.shape[0]

    def block(by):
        py = lax.rem(y + by, 4)
        at = pl.ds(pl.multiple_of(lax.div(py, 2) * rows, 16), rows)
        lanes = pl.ds(pl.multiple_of(lax.rem(py, 2) * half, 128), half)
        return own[at, lanes] + prev[at, lanes].astype(f32) + following[at, lanes].astype(f32)

    v_prev, v_next, v_far = (from_parts(part[part.shape[0] - 32 :, :]) for part in (low, high, prev))
    total = (vector[...] + v_far) + (v_prev + v_next)
    laid[...] = jnp.zeros_like(laid)
    for r in range(5):
        for k in range(2):
            laid[2 * r + k : 2 * r + k + 1, :] = total[r : r + 1, k * half : (k + 1) * half]
    top = laid[...].astype(bf16)
    riding = jnp.concatenate([top, (laid[...] - top.astype(f32)).astype(bf16)], 0)
    sums[...] = from_parts(riding)
    mine[...] = block(0)
    for by, to in ((1, ahead), (2, far), (3, behind)):
        to[:rows, :] = block(by).astype(bf16)
        to[rows:, :] = riding


def finish_expand_kernel(own, prev, following, mine, ahead, far, behind):
    x, _ = place()
    rows = mine.shape[0]

    def block(by):
        at = pl.ds(pl.multiple_of(lax.rem(x + by, 4) * rows, 16), rows)
        return own[at, :] + prev[at, :].astype(f32) + following[at, :].astype(f32)

    mine[...] = block(0)
    for by, to in ((1, ahead), (2, far), (3, behind)):
        to[...] = block(by).astype(bf16)


def middle_kernel(mine, ahead, behind, total):
    total[...] = mine[...] + ahead[...].astype(f32) + behind[...].astype(f32)


def last_kernel(mine, *refs):
    if len(refs) == 3:
        got, (kept, given) = refs[:1], refs[1:]
    else:
        got, own, (kept, given, sums) = refs[:3], refs[3], refs[4:]
        v_ahead, v_far, v_behind = (from_parts(part[part.shape[0] - 32 :, :]) for part in got)
        sums[...] = (own[...] + v_far) + (v_ahead + v_behind)
    rows = mine.shape[0]
    total = mine[...]
    for part in got:
        total = total + part[:rows, :].astype(f32)
    core = lax.axis_index("core")
    top, bottom = total[: rows // 2], total[rows // 2 :]
    kept[...] = jnp.where(core == 0, top, bottom)
    given[...] = jnp.where(core == 0, bottom, top)


def inputs_kernel(inputs, upstream, grad, gain, result):
    tokens, width = inputs.shape

    def step(i, _):
        at = pl.ds(pl.multiple_of(i * 32, 32), 32)
        features = inputs[at, :].astype(f32)
        shifted = features - jnp.mean(features, axis=1, keepdims=True)
        scale = lax.rsqrt(jnp.mean(shifted * shifted, axis=1, keepdims=True) + EPSILON)
        normed = shifted * scale
        weighted = grad[at, :].astype(f32) * gain[...]
        mean_one = jnp.mean(weighted, axis=1, keepdims=True)
        mean_two = jnp.mean(weighted * normed, axis=1, keepdims=True)
        change = scale * (weighted - mean_one - normed * mean_two)
        result[at, :] = (upstream[at, :].astype(f32) + change).astype(bf16)
        return 0

    lax.fori_loop(0, tokens // 32, step, 0)


def rows_kernel(near, other, near_centre, other_centre, near_scale, other_scale, back, expand, mine, others, sums):
    tokens, width = near.shape[2:]

    def tile_of(lanes):
        gain = plain = 0.0
        for half, part, centre, scale in ((1, other, other_centre, other_scale), (0, near, near_centre, near_scale)):
            rows = dot(back[pl.ds(half * 4 * tokens, 4 * tokens), :], expand[lanes, :], ((1,), (1,)))
            features = jnp.concatenate([part[k, 0, :, lanes] for k in range(4)], 0).astype(f32)
            normed = (features - centre[...]) * scale[...]
            gain = gain + jnp.sum(rows * normed, axis=0, keepdims=True)
            plain = plain + jnp.sum(rows, axis=0, keepdims=True)
            if half:
                others[:, lanes] = rows.astype(bf16)
            else:
                mine[:, lanes] = rows
        sums[0:1, lanes] = gain
        sums[1:2, lanes] = plain

    def step(j, _):
        tile_of(pl.ds(pl.multiple_of(j * 256, 256), 256))
        return 0

    whole = width // 256
    lax.fori_loop(0, whole, step, 0)
    if width % 256:
        tile_of(slice(whole * 256, width))


def local(inputs, upstream, norm_gain, norm_shift, expand_weight, expand_bias, shrink_weight):
    tokens, width = inputs.shape
    rows, hidden = expand_weight.shape
    half = hidden // 2
    x, ylo, z, yhi, core = (lax.axis_index(name) for name in AXES)
    y = 2 * yhi + ylo

    def by_core(weight):
        kept = lax.dynamic_slice_in_dim(weight, core * half, half, 1)
        given = lax.dynamic_slice_in_dim(weight, (1 - core) * half, half, 1)
        got = swap(given)
        return jnp.where(core == 0, jnp.concatenate([kept, got], 0), jnp.concatenate([got, kept], 0))

    block_rows = 2 * rows

    bias_near = lax.ppermute(expand_bias, "ylo", [(0, 1), (1, 0)])
    a, b = by_core(expand_weight), by_core(shrink_weight)

    (stacked,) = call(stack_kernel, [((1, 2, tokens, width), bf16)], (inputs, upstream))
    near = lax.all_gather(stacked, "z", axis=0, tiled=True)

    (a_left, a_right), (b_left, b_right) = both_ways(a, a, "x"), both_ways(b, b, "y")
    a_low, a_high = both_ways(a_left[:rows], a_right[rows:], "x")
    b_low, b_high = both_ways(b_left[:rows], b_right[rows:], "y")
    a = jnp.concatenate([a, a_right, a_low, a_high, a_left], 0)
    a, bias_near = lax.optimization_barrier((a, bias_near))
    b = jnp.concatenate([b, b_right, b_low, b_high, b_left], 0)
    (a_left, a_right), (b_left, b_right) = both_ways(a, a, "y"), both_ways(b, b, "x")
    halves = a_left[: 2 * block_rows], a_right[2 * block_rows :], b_left[: 2 * block_rows], b_right[2 * block_rows :]
    a_low, a_high = both_ways(*halves[:2], "y")
    b_low, b_high = both_ways(*halves[2:], "x")
    pieces = (a, a_right, a_low, a_high, a_left), (b, b_right, b_low, b_high, b_left)
    bias_both = jnp.where(ylo == 0, jnp.stack([expand_bias, bias_near]), jnp.stack([bias_near, expand_bias]))
    bias_own = lax.dynamic_slice_in_dim(bias_both, core * half, half, 1).reshape(1, 2 * half)

    (expand_all, first_mark), (shrink_all, second_mark) = (
        call(functools.partial(assemble_kernel, first), [((width, 2 * half), bf16)], part, mark=True)
        for first, part in zip("xy", pieces, strict=True)
    )
    near, first_mark, second_mark = lax.optimization_barrier((near, first_mark, second_mark))
    other = swap(near)
    many = 8 * tokens
    tall, wide = ((width, many), bf16), ((many, 2 * half), bf16)
    column, half_tall, bias_row = ((4 * tokens, 1), f32), (4 * tokens, width), ((1, 2 * half), f32)
    gain, shift_by = norm_gain[None], norm_shift[None]
    tile = pltpu.VMEM((2, 4 * tokens, 256), f32)
    turned = pltpu.VMEM((width, 4 * tokens), bf16)
    normed, near_centre, near_scale, normed_t, up_t = call(
        functools.partial(norm_kernel, 0, unroll=True),
        [(half_tall, bf16), column, column, tall, tall],
        (near, gain, shift_by),
        scratch=[turned],
        behind=(first_mark, second_mark),
    )
    near_bias, active, back = call(
        functools.partial(hidden_kernel, 0, unroll=True),
        [bias_row, wide, wide],
        (near, normed, expand_all, shrink_all, bias_own),
        scratch=[tile, tile],
    )
    other_centre, other_scale, normed_t, up_t, other_bias, active, back = call(
        second_kernel,
        [column, column, tall, tall, bias_row, wide, wide],
        (other, gain, shift_by, bias_own, expand_all, shrink_all, normed_t, up_t, active, back),
        scratch=[pltpu.VMEM(half_tall, bf16), turned, tile, tile],
        aliases={6: 2, 7: 3, 8: 5, 9: 6},
    )
    bias_part = near_bias + other_bias

    mine, others, norm_sums = call(
        rows_kernel,
        [((4 * tokens, width), f32), ((4 * tokens, width), bf16), ((2, width), f32)],
        (near, other, near_centre, other_centre, near_scale, other_scale, back, expand_all),
    )

    short, long = ((block_rows + 32, 2 * half), bf16), ((2 * block_rows, half), bf16)
    s_low, s_high, e_low, e_high, vector = call(
        far_kernel,
        [short, short, long, long, ((16, 2 * half), f32)],
        (up_t, active, normed_t, back, norm_sums, bias_part),
    )
    (s_low, s_high), (e_low, e_high) = both_ways(s_low, s_high, "x"), both_ways(e_low, e_high, "y")

    both, mark = call(add_kernel, [((4 * tokens, width), bf16)], (mine, swap(others)), behind=(vector,), mark=True)

    s_wide, e_wide = (2 * block_rows, 2 * half), (4 * block_rows, half)
    s_own, e_own, s_terms, e_terms = call(
        near_kernel,
        [(s_wide, f32), (e_wide, f32), ((2, *s_wide), f32), ((2, *e_wide), f32)],
        (up_t, active, normed_t, back),
        behind=(mark,),
    )
    s_ahead, s_behind, e_ahead, e_behind, mark = call(
        pass_kernel,
        [((2 * block_rows + 32, 2 * half), bf16), (s_wide, bf16), (e_wide, bf16), (e_wide, bf16)],
        (s_terms, e_terms, s_low, s_high, e_low, e_high),
        mark=True,
    )
    (s_prev, s_next), (e_prev, e_next) = both_ways(s_ahead, s_behind, "x"), both_ways(e_ahead, e_behind, "y")

    both, pass_mark = lax.optimization_barrier((both, mark))
    grad_normed = lax.psum_scatter(both, "z", scatter_dimension=0, tiled=True)

    block, riding = (block_rows, half), ((block_rows + 32, half), bf16)
    s_mine, *s_blocks, vector = call(
        finish_shrink_kernel,
        [(block, f32), riding, riding, riding, ((16, half), f32)],
        (s_own, s_prev, s_next, s_low, s_high, vector),
        scratch=[pltpu.VMEM((16, half), f32)],
        behind=(pass_mark,),
    )
    s_got = direct(*s_blocks, "y")
    e_mine, *e_blocks = call(finish_expand_kernel, [(block, f32)] + [(block, bf16)] * 3, (e_own, e_prev, e_next))
    e_ahead, e_far, e_behind = direct(*e_blocks, "x")
    inputs_grad, done = call(
        inputs_kernel, [((tokens, width), bf16)], (inputs, upstream, grad_normed, norm_gain[None]), mark=True
    )
    e_mine, mark = call(middle_kernel, [(block, f32)], (e_mine, e_ahead, e_far), behind=(done,), mark=True)
    part = ((rows, half), f32)
    s_kept, s_given, vector = call(last_kernel, [part, part, ((16, half), f32)], (s_mine, *s_got, vector), behind=(mark,))
    e_kept, e_given = call(last_kernel, [part, part], (e_mine, e_behind))

    def by_rows(kept, given):
        got = swap(given)
        return jnp.where(core == 0, jnp.concatenate([kept, got], 1), jnp.concatenate([got, kept], 1))

    shrink_grad, expand_grad = by_rows(s_kept, s_given), by_rows(e_kept, e_given)
    norm_sums = pair_sum(vector[:8], "z")
    norm_sums = norm_sums + swap(norm_sums)
    gain_grad, shift_grad = (norm_sums[i : i + 4].reshape(-1)[:width] for i in (0, 4))
    bias_mine = lax.dynamic_index_in_dim(vector, 8 + ylo, 0, keepdims=False)
    bias_other = swap(bias_mine)
    bias_grad = jnp.where(
        core == 0, jnp.concatenate([bias_mine, bias_other]), jnp.concatenate([bias_other, bias_mine])
    )
    return inputs_grad, gain_grad, shift_grad, expand_grad, bias_grad, shrink_grad


def solution(mesh):
    fine = Mesh(mesh.devices.reshape(4, 2, 4, 2, 2), AXES)
    by_token = P(AXES, None)
    by_weight = P(("x", "yhi", "core"), ("ylo", "z"))
    by_hidden = P(("ylo", "z"))
    return jax.shard_map(
        local,
        mesh=fine,
        in_specs=(by_token, by_token, P(), P(), by_weight, by_hidden, by_weight),
        out_specs=(by_token, P(), P(), by_weight, by_hidden, by_weight),
        check_vma=False,
    )
```

```python
import functools

import jax
import jax.numpy as jnp
from jax import lax
from jax.experimental import pallas as pl
from jax.experimental.pallas import tpu as pltpu
from jax.sharding import Mesh, PartitionSpec as P

EPSILON = 1e-06
ROOT_HALF = 0.7071067811865476
INV_ROOT_TWO_PI = 0.3989422804014327

AXES = ("x", "ylo", "z", "yhi", "core")
PLANE_Y = ("ylo", "yhi")
f32, bf16 = jnp.float32, jnp.bfloat16


def y_index(y):
    return (y % 2) * 2 + y // 2


def shift(value, axis, by):
    if axis == "y":
        pairs = [(y_index(y), y_index((y + by) % 4)) for y in range(4)]
        return lax.ppermute(value, PLANE_Y, pairs)
    return lax.ppermute(value, axis, [(i, (i + by) % 4) for i in range(4)])


def swap(value):
    return lax.ppermute(value, "core", [(0, 1), (1, 0)])


def after(value, *others):
    return lax.optimization_barrier((value, *others))[0]


def both_ways(ahead, behind, axis):
    return shift(ahead, axis, 1), shift(behind, axis, -1)


def pair_sum(value, axis):
    for bit in (1, 2):
        value = value + lax.ppermute(value, axis, [(i, i ^ bit) for i in range(4)])
    return value


def from_parts(rows):
    return rows[:16].astype(f32) + rows[16:].astype(f32)


def direct(ahead, far, behind, axis):
    return shift(ahead, axis, 1), shift(far, axis, 2), shift(behind, axis, 3)


def assemble_kernel(first, own, right, far_low, far_high, left, whole):
    x, y = place()
    rows, half = own.shape[0] // 4, own.shape[1]
    for far_second in range(4):
        for far_first in range(4):
            if far_second == 2:
                bundle, at = (far_low, far_first) if far_first < 2 else (far_high, far_first - 2)
            else:
                bundle, at = {0: own, 1: right, 3: left}[far_second], far_first
            far_x, far_y = (far_first, far_second) if first == "x" else (far_second, far_first)
            px, py = lax.rem(x + far_x, 4), lax.rem(y + far_y, 4)
            row = pl.multiple_of((2 * px + lax.div(py, 2)) * rows, 16)
            column = pl.multiple_of(lax.rem(py, 2) * half, 128)
            whole[pl.ds(row, rows), pl.ds(column, half)] = bundle[at * rows : (at + 1) * rows, :]


def place():
    return lax.axis_index("x"), 2 * lax.axis_index("yhi") + lax.axis_index("ylo")


def gelu_parts(pre):
    cdf = 0.5 * (1.0 + lax.erf(pre * ROOT_HALF))
    density = INV_ROOT_TWO_PI * jnp.exp(-0.5 * pre * pre)
    return pre * cdf, cdf + pre * density


def dot(left, right, dims=((1,), (0,))):
    return lax.dot_general(left, right, (dims, ((), ())), preferred_element_type=f32)


def call(kernel, outs, args, scratch=(), aliases=None, behind=(), mark=False, limit=16):
    given, made = len(args), len(outs)

    def body(*refs):
        refs = refs[:given] + refs[given + len(behind) :]
        if mark:
            refs[given + made][...] = jnp.zeros_like(refs[given + made])
            refs = refs[: given + made] + refs[given + made + 1 :]
        kernel(*refs)

    outs = [*outs, *[((8, 128), f32)] * mark]
    whole = pl.BlockSpec(memory_space=pltpu.VMEM)
    return pl.pallas_call(
        body,
        out_shape=[jax.ShapeDtypeStruct(shape, dtype) for shape, dtype in outs],
        in_specs=[whole] * (given + len(behind)),
        out_specs=[whole] * len(outs),
        scratch_shapes=list(scratch),
        input_output_aliases=aliases or {},
        compiler_params=pltpu.CompilerParams(vmem_limit_bytes=limit * 2**20),
        cost_estimate=pl.CostEstimate(flops=10**6, bytes_accessed=10**6, transcendentals=0),
    )(*args, *behind)


def stack_kernel(inputs, upstream, stacked):
    stacked[0, 0] = inputs[...]
    stacked[0, 1] = upstream[...]


def add_kernel(mine, others, total):
    def step(i, _):
        at = pl.ds(pl.multiple_of(i * 32, 32), 32)
        total[at, :] = (mine[at, :] + others[at, :].astype(f32)).astype(bf16)
        return 0

    lax.fori_loop(0, mine.shape[0] // 32, step, 0)


def norm_kernel(half, part, gain, shift_by, *refs, unroll=False):
    normed, centre, scale, normed_t, up_t, turned = refs[-6:]
    tokens, width = part.shape[2:]
    to, rows = pl.ds(half * 4 * tokens, 4 * tokens), width // 8

    def normalise(k, _):
        at = pl.ds(pl.multiple_of(k * tokens, 16), tokens)
        features = part[k, 0].astype(f32)
        mean = jnp.mean(features, axis=1, keepdims=True)
        shifted = features - mean
        inv = lax.rsqrt(jnp.mean(shifted * shifted, axis=1, keepdims=True) + EPSILON)
        normed[at, :] = (shifted * inv * gain[...] + shift_by[...]).astype(bf16)
        centre[at, :] = mean
        scale[at, :] = inv
        return 0

    def turn(c, _):
        lanes = pl.ds(pl.multiple_of(c * 128, 128), 128)
        up_t[lanes, to] = jnp.concatenate([part[k, 1, :, lanes] for k in range(4)], 0).T
        turned[lanes, :] = normed[:, lanes].T
        return 0

    def order(b, _):
        at = pl.multiple_of((lax.rem(b, 2) * 4 + lax.div(b, 2)) * rows, 16)
        normed_t[pl.ds(at, rows), to] = turned[pl.ds(pl.multiple_of(b * rows, 16), rows), :]
        return 0

    lax.fori_loop(0, 4, normalise, 0, unroll=unroll)
    lax.fori_loop(0, width // 128, turn, 0, unroll=unroll)
    lax.fori_loop(0, 8, order, 0, unroll=unroll)


def hidden_kernel(half, part, normed, expand, shrink, bias, *refs, unroll=False):
    bias_sum, active, back, pre_tile, back_tile = refs[-5:]
    tokens, width = part.shape[2:]
    tile, to = 256, pl.ds(half * 4 * tokens, 4 * tokens)
    tiles = expand.shape[1] // tile

    def lanes_of(j):
        return slice(j * tile, (j + 1) * tile) if unroll else pl.ds(pl.multiple_of(j * tile, tile), tile)

    def products(j, slot):
        lanes = lanes_of(j)
        pre_tile[slot] = dot(normed[...], expand[:, lanes])
        back_tile[slot] = dot(jnp.concatenate([part[k, 1] for k in range(4)], 0), shrink[:, lanes])

    def finish(j, slot):
        lanes = lanes_of(j)
        value, slope = gelu_parts(pre_tile[slot] + bias[:, lanes])
        active[to, lanes] = value.astype(bf16)
        grad = (back_tile[slot] * slope).astype(bf16)
        back[to, lanes] = grad
        bias_sum[:, lanes] = jnp.sum(grad.astype(f32), axis=0, keepdims=True)

    def step(j, _):
        products(j, 0)
        finish(j, 0)
        return 0

    if unroll:
        products(0, 0)
        for j in range(1, tiles):
            products(j, j % 2)
            finish(j - 1, (j - 1) % 2)
        finish(tiles - 1, (tiles - 1) % 2)
    else:
        lax.fori_loop(0, tiles, step, 0)


def second_kernel(part, gain, shift_by, bias, expand, shrink, normed_t_in, up_t_in, active_in, back_in, *refs):
    centre, scale, normed_t, up_t, bias_sum, active, back, normed, turned, pre_tile, back_tile = refs
    norm_kernel(1, part, gain, shift_by, normed, centre, scale, normed_t, up_t, turned)
    hidden_kernel(1, part, normed, expand, shrink, bias, bias_sum, active, back, pre_tile, back_tile)


def shrink_tile(far, n, up_t, active):
    x, _ = place()
    rows, lanes = up_t.shape[0] // 4, pl.ds(pl.multiple_of(n * 256, 256), 256)
    return lanes, dot(up_t[pl.ds(pl.multiple_of(lax.rem(x + far, 4) * rows, 16), rows), :], active[:, lanes])


def expand_tile(far, n, normed_t, back):
    _, y = place()
    py = lax.rem(y + far, 4)
    rows, half = normed_t.shape[0] // 2, back.shape[1] // 2
    right = back[:, pl.ds(pl.multiple_of(lax.rem(py, 2) * half + n * 256, 256), 256)]
    left = normed_t[pl.ds(pl.multiple_of(lax.div(py, 2) * rows, 16), rows), :]
    return pl.ds(pl.multiple_of(n * 256, 256), 256), dot(left, right)


def far_kernel(up_t, active, normed_t, back, sums, bias, shrink_low, shrink_high, expand_low, expand_high, vector):
    def tile_of(make, left, right, low, high):
        def step(n, _):
            lanes, term = make(2, n, left, right)
            rows = term.shape[0] // 2
            low[pl.ds(0, rows), lanes] = term[:rows].astype(bf16)
            high[pl.ds(0, rows), lanes] = term[rows:].astype(bf16)
            return 0

        return step

    lax.fori_loop(0, active.shape[1] // 256, tile_of(shrink_tile, up_t, active, shrink_low, shrink_high), 0)
    lax.fori_loop(0, back.shape[1] // 512, tile_of(expand_tile, normed_t, back, expand_low, expand_high), 0)
    hidden, width = bias.shape[1], sums.shape[1]
    vector[...] = jnp.zeros_like(vector)
    for i in range(2):
        for j, start in enumerate(range(0, width, hidden)):
            size = min(hidden, width - start)
            vector[2 * i + j : 2 * i + j + 1, :size] = sums[i : i + 1, start : start + size]
    vector[4:5, :] = bias[...]
    high = vector[...].astype(bf16)
    riding = jnp.concatenate([high, (vector[...] - high.astype(f32)).astype(bf16)], 0)
    for to in (shrink_low, shrink_high):
        to[to.shape[0] - 32 :, :] = riding
    vector[...] = riding[:16].astype(f32) + riding[16:].astype(f32)


def near_kernel(up_t, active, normed_t, back, shrink_own, expand_own, shrink_terms, expand_terms):
    def tile_of(make, left, right, own, terms):
        def for_own(n, _):
            lanes, term = make(0, n, left, right)
            own[:, lanes] = term
            return 0

        def for_others(i, _):
            d, n = lax.rem(i, 2), lax.div(i, 2)
            lanes, term = make(1 + 2 * d, n, left, right)
            terms[d, :, lanes] = term
            return 0

        return for_own, for_others

    for make, left, right, own, terms in (
        (shrink_tile, up_t, active, shrink_own, shrink_terms),
        (expand_tile, normed_t, back, expand_own, expand_terms),
    ):
        tiles = own.shape[1] // 256
        for_own, for_others = tile_of(make, left, right, own, terms)
        lax.fori_loop(0, 2 * tiles, for_others, 0)
        lax.fori_loop(0, tiles, for_own, 0)


def pass_kernel(s_terms, e_terms, s_low, s_high, e_low, e_high, s_ahead, s_behind, e_ahead, e_behind):
    for terms, low, high, ahead, behind in (
        (s_terms, s_low, s_high, s_ahead, s_behind),
        (e_terms, e_low, e_high, e_ahead, e_behind),
    ):
        rows = terms.shape[1] // 2

        def step(i, _, rows=rows, terms=terms, low=low, high=high, ahead=ahead, behind=behind):
            at, then = pl.ds(pl.multiple_of(i * 16, 16), 16), pl.ds(pl.multiple_of(rows + i * 16, 16), 16)
            ahead[at, :] = (terms[0, at, :] + low[at, :].astype(f32)).astype(bf16)
            ahead[then, :] = terms[0, then, :].astype(bf16)
            behind[at, :] = terms[1, at, :].astype(bf16)
            behind[then, :] = (terms[1, then, :] + high[at, :].astype(f32)).astype(bf16)
            return 0

        lax.fori_loop(0, rows // 16, step, 0)
    rows = s_terms.shape[1]
    s_ahead[rows:, :] = s_low[rows // 2 :, :]


def finish_shrink_kernel(own, prev, following, low, high, vector, mine, ahead, far, behind, sums, laid):
    _, y = place()
    rows, half = mine.shape
    wide = own.shape[0]

    def block(by):
        py = lax.rem(y + by, 4)
        at = pl.ds(pl.multiple_of(lax.div(py, 2) * rows, 16), rows)
        lanes = pl.ds(pl.multiple_of(lax.rem(py, 2) * half, 128), half)
        return own[at, lanes] + prev[at, lanes].astype(f32) + following[at, lanes].astype(f32)

    v_prev, v_next, v_far = (from_parts(part[part.shape[0] - 32 :, :]) for part in (low, high, prev))
    total = (vector[...] + v_far) + (v_prev + v_next)
    laid[...] = jnp.zeros_like(laid)
    for r in range(5):
        for k in range(2):
            laid[2 * r + k : 2 * r + k + 1, :] = total[r : r + 1, k * half : (k + 1) * half]
    top = laid[...].astype(bf16)
    riding = jnp.concatenate([top, (laid[...] - top.astype(f32)).astype(bf16)], 0)
    sums[...] = from_parts(riding)
    mine[...] = block(0)
    for by, to in ((1, ahead), (2, far), (3, behind)):
        to[:rows, :] = block(by).astype(bf16)
        to[rows:, :] = riding


def finish_expand_kernel(own, prev, following, mine, ahead, far, behind):
    x, _ = place()
    rows = mine.shape[0]

    def block(by):
        at = pl.ds(pl.multiple_of(lax.rem(x + by, 4) * rows, 16), rows)
        return own[at, :] + prev[at, :].astype(f32) + following[at, :].astype(f32)

    mine[...] = block(0)
    for by, to in ((1, ahead), (2, far), (3, behind)):
        to[...] = block(by).astype(bf16)


def middle_kernel(mine, ahead, behind, total):
    total[...] = mine[...] + ahead[...].astype(f32) + behind[...].astype(f32)


def last_kernel(mine, *refs):
    if len(refs) == 3:
        got, (kept, given) = refs[:1], refs[1:]
    else:
        got, own, (kept, given, sums) = refs[:3], refs[3], refs[4:]
        v_ahead, v_far, v_behind = (from_parts(part[part.shape[0] - 32 :, :]) for part in got)
        sums[...] = (own[...] + v_far) + (v_ahead + v_behind)
    rows = mine.shape[0]
    total = mine[...]
    for part in got:
        total = total + part[:rows, :].astype(f32)
    core = lax.axis_index("core")
    top, bottom = total[: rows // 2], total[rows // 2 :]
    kept[...] = jnp.where(core == 0, top, bottom)
    given[...] = jnp.where(core == 0, bottom, top)


def join_kernel(kept, got, whole):
    half, core = kept.shape[1], lax.axis_index("core")
    whole[:, :half] = jnp.where(core == 0, kept[...], got[...])
    whole[:, half:] = jnp.where(core == 0, got[...], kept[...])


def norm_sums_kernel(own, others, gain, plain):
    for first, to in ((0, gain), (4, plain)):
        for r in range(to.shape[0]):
            at = slice(first + r // 4, first + r // 4 + 1), slice(r % 4 * 128, r % 4 * 128 + 128)
            to[r : r + 1, :] = own[at] + others[at]


def inputs_kernel(inputs, upstream, grad, gain, result):
    tokens, width = inputs.shape

    def step(i, _):
        at = pl.ds(pl.multiple_of(i * 32, 32), 32)
        features = inputs[at, :].astype(f32)
        shifted = features - jnp.mean(features, axis=1, keepdims=True)
        scale = lax.rsqrt(jnp.mean(shifted * shifted, axis=1, keepdims=True) + EPSILON)
        normed = shifted * scale
        weighted = grad[at, :].astype(f32) * gain[...]
        mean_one = jnp.mean(weighted, axis=1, keepdims=True)
        mean_two = jnp.mean(weighted * normed, axis=1, keepdims=True)
        change = scale * (weighted - mean_one - normed * mean_two)
        result[at, :] = (upstream[at, :].astype(f32) + change).astype(bf16)
        return 0

    lax.fori_loop(0, tokens // 32, step, 0)


def rows_kernel(near, other, near_centre, other_centre, near_scale, other_scale, back, expand, mine, others, sums):
    tokens, width = near.shape[2:]

    def tile_of(lanes):
        gain = plain = 0.0
        for half, part, centre, scale in ((1, other, other_centre, other_scale), (0, near, near_centre, near_scale)):
            rows = dot(back[pl.ds(half * 4 * tokens, 4 * tokens), :], expand[lanes, :], ((1,), (1,)))
            features = jnp.concatenate([part[k, 0, :, lanes] for k in range(4)], 0).astype(f32)
            normed = (features - centre[...]) * scale[...]
            gain = gain + jnp.sum(rows * normed, axis=0, keepdims=True)
            plain = plain + jnp.sum(rows, axis=0, keepdims=True)
            if half:
                others[:, lanes] = rows.astype(bf16)
            else:
                mine[:, lanes] = rows
        sums[0:1, lanes] = gain
        sums[1:2, lanes] = plain

    def step(j, _):
        tile_of(pl.ds(pl.multiple_of(j * 256, 256), 256))
        return 0

    whole = width // 256
    lax.fori_loop(0, whole, step, 0)
    if width % 256:
        tile_of(slice(whole * 256, width))


def local(inputs, upstream, norm_gain, norm_shift, expand_weight, expand_bias, shrink_weight):
    tokens, width = inputs.shape
    rows, hidden = expand_weight.shape
    half = hidden // 2
    x, ylo, z, yhi, core = (lax.axis_index(name) for name in AXES)
    y = 2 * yhi + ylo

    def by_core(weight):
        kept = lax.dynamic_slice_in_dim(weight, core * half, half, 1)
        given = lax.dynamic_slice_in_dim(weight, (1 - core) * half, half, 1)
        got = swap(given)
        return jnp.where(core == 0, jnp.concatenate([kept, got], 0), jnp.concatenate([got, kept], 0))

    block_rows = 2 * rows

    bias_near = lax.ppermute(expand_bias, "ylo", [(0, 1), (1, 0)])
    a, b = by_core(expand_weight), by_core(shrink_weight)

    (stacked,) = call(stack_kernel, [((1, 2, tokens, width), bf16)], (inputs, upstream))
    near = lax.all_gather(stacked, "z", axis=0, tiled=True)

    (a_left, a_right), (b_left, b_right) = both_ways(a, a, "x"), both_ways(b, b, "y")
    a_low, a_high = both_ways(a_left[:rows], a_right[rows:], "x")
    b_low, b_high = both_ways(b_left[:rows], b_right[rows:], "y")
    a = jnp.concatenate([a, a_right, a_low, a_high, a_left], 0)
    a, bias_near = lax.optimization_barrier((a, bias_near))
    b = jnp.concatenate([b, b_right, b_low, b_high, b_left], 0)
    (a_left, a_right), (b_left, b_right) = both_ways(a, a, "y"), both_ways(b, b, "x")
    halves = a_left[: 2 * block_rows], a_right[2 * block_rows :], b_left[: 2 * block_rows], b_right[2 * block_rows :]
    a_low, a_high = both_ways(*halves[:2], "y")
    b_low, b_high = both_ways(*halves[2:], "x")
    pieces = (a, a_right, a_low, a_high, a_left), (b, b_right, b_low, b_high, b_left)
    bias_both = jnp.where(ylo == 0, jnp.stack([expand_bias, bias_near]), jnp.stack([bias_near, expand_bias]))
    bias_own = lax.dynamic_slice_in_dim(bias_both, core * half, half, 1).reshape(1, 2 * half)

    (expand_all, first_mark), (shrink_all, second_mark) = (
        call(functools.partial(assemble_kernel, first), [((width, 2 * half), bf16)], part, mark=True)
        for first, part in zip("xy", pieces, strict=True)
    )
    near, first_mark, second_mark = lax.optimization_barrier((near, first_mark, second_mark))
    other = swap(near)
    many = 8 * tokens
    tall, wide = ((width, many), bf16), ((many, 2 * half), bf16)
    column, half_tall, bias_row = ((4 * tokens, 1), f32), (4 * tokens, width), ((1, 2 * half), f32)
    gain, shift_by = norm_gain[None], norm_shift[None]
    tile = pltpu.VMEM((2, 4 * tokens, 256), f32)
    turned = pltpu.VMEM((width, 4 * tokens), bf16)
    normed, near_centre, near_scale, normed_t, up_t = call(
        functools.partial(norm_kernel, 0, unroll=True),
        [(half_tall, bf16), column, column, tall, tall],
        (near, gain, shift_by),
        scratch=[turned],
        behind=(first_mark, second_mark),
    )
    near_bias, active, back = call(
        functools.partial(hidden_kernel, 0, unroll=True),
        [bias_row, wide, wide],
        (near, normed, expand_all, shrink_all, bias_own),
        scratch=[tile, tile],
    )
    other_centre, other_scale, normed_t, up_t, other_bias, active, back = call(
        second_kernel,
        [column, column, tall, tall, bias_row, wide, wide],
        (other, gain, shift_by, bias_own, expand_all, shrink_all, normed_t, up_t, active, back),
        scratch=[pltpu.VMEM(half_tall, bf16), turned, tile, tile],
        aliases={6: 2, 7: 3, 8: 5, 9: 6},
    )
    bias_part = near_bias + other_bias

    mine, others, norm_sums = call(
        rows_kernel,
        [((4 * tokens, width), f32), ((4 * tokens, width), bf16), ((2, width), f32)],
        (near, other, near_centre, other_centre, near_scale, other_scale, back, expand_all),
    )

    short, long = ((block_rows + 32, 2 * half), bf16), ((2 * block_rows, half), bf16)
    s_low, s_high, e_low, e_high, vector = call(
        far_kernel,
        [short, short, long, long, ((16, 2 * half), f32)],
        (up_t, active, normed_t, back, norm_sums, bias_part),
    )
    (s_low, s_high), (e_low, e_high) = both_ways(s_low, s_high, "x"), both_ways(e_low, e_high, "y")

    both, mark = call(add_kernel, [((4 * tokens, width), bf16)], (mine, swap(others)), behind=(vector,), mark=True)

    s_wide, e_wide = (2 * block_rows, 2 * half), (4 * block_rows, half)
    s_own, e_own, s_terms, e_terms = call(
        near_kernel,
        [(s_wide, f32), (e_wide, f32), ((2, *s_wide), f32), ((2, *e_wide), f32)],
        (up_t, active, normed_t, back),
        behind=(mark,),
    )
    s_ahead, s_behind, e_ahead, e_behind, mark = call(
        pass_kernel,
        [((2 * block_rows + 32, 2 * half), bf16), (s_wide, bf16), (e_wide, bf16), (e_wide, bf16)],
        (s_terms, e_terms, s_low, s_high, e_low, e_high),
        mark=True,
    )
    (s_prev, s_next), (e_prev, e_next) = both_ways(s_ahead, s_behind, "x"), both_ways(e_ahead, e_behind, "y")

    both, pass_mark = lax.optimization_barrier((both, mark))
    grad_normed = lax.psum_scatter(both, "z", scatter_dimension=0, tiled=True)

    block, riding = (block_rows, half), ((block_rows + 32, half), bf16)
    s_mine, *s_blocks, vector = call(
        finish_shrink_kernel,
        [(block, f32), riding, riding, riding, ((16, half), f32)],
        (s_own, s_prev, s_next, s_low, s_high, vector),
        scratch=[pltpu.VMEM((16, half), f32)],
        behind=(pass_mark,),
    )
    s_got = direct(*s_blocks, "y")
    e_mine, *e_blocks = call(finish_expand_kernel, [(block, f32)] + [(block, bf16)] * 3, (e_own, e_prev, e_next))
    e_ahead, e_far, e_behind = direct(*e_blocks, "x")
    inputs_grad, done = call(
        inputs_kernel, [((tokens, width), bf16)], (inputs, upstream, grad_normed, norm_gain[None]), mark=True
    )
    e_mine, mark = call(middle_kernel, [(block, f32)], (e_mine, e_ahead, e_far), behind=(done,), mark=True)
    part = ((rows, half), f32)
    s_kept, s_given, vector = call(last_kernel, [part, part, ((16, half), f32)], (s_mine, *s_got, vector), behind=(mark,))
    e_kept, e_given = call(last_kernel, [part, part], (e_mine, e_behind))

    def by_rows(kept, given):
        return call(join_kernel, [((rows, 2 * half), f32)], (kept, swap(given)))[0]

    shrink_grad, expand_grad = by_rows(s_kept, s_given), by_rows(e_kept, e_given)
    norm_sums = pair_sum(vector[:8], "z")
    lines = ((width // 128, 128), f32)
    gain_grad, shift_grad = (
        part.reshape(width) for part in call(norm_sums_kernel, [lines, lines], (norm_sums, swap(norm_sums)))
    )
    bias_mine = lax.dynamic_index_in_dim(vector, 8 + ylo, 0, keepdims=False)
    bias_other = swap(bias_mine)
    bias_grad = jnp.where(
        core == 0, jnp.concatenate([bias_mine, bias_other]), jnp.concatenate([bias_other, bias_mine])
    )
    return inputs_grad, gain_grad, shift_grad, expand_grad, bias_grad, shrink_grad


def solution(mesh):
    fine = Mesh(mesh.devices.reshape(4, 2, 4, 2, 2), AXES)
    by_token = P(AXES, None)
    by_weight = P(("x", "yhi", "core"), ("ylo", "z"))
    by_hidden = P(("ylo", "z"))
    return jax.shard_map(
        local,
        mesh=fine,
        in_specs=(by_token, by_token, P(), P(), by_weight, by_hidden, by_weight),
        out_specs=(by_token, P(), P(), by_weight, by_hidden, by_weight),
        check_vma=False,
    )
```
